256 devices in a mesh: patch: 64 (over x, z, core), visit: 4 (over y).
Axes of the slice: x: 4, y: 4, z: 8, core: 2. Of those that a mesh axis runs over, the one named last changes fastest.
Arguments:
- image: float32 [4, 1536, 128, 128], P('visit', 'patch'), may hold values from -6 to 6
- variance: float32 [4, 1536, 128, 128], P('visit', 'patch'), may hold values from 0.01 to 3600, as said below
- patches: int32 [4, 1536, 2], P('visit', 'patch'), may hold values from 0 to 63, all different within a row; in each aligned block of 24 rows (0 to 23, 24 to 47, ..., all dimensions but the last counted through in order) at most 2 rows name the same one
- offsets: int32 [4, 1536, 2, 2], P('visit', 'patch'), may hold values from -64 to 192
- psf_index: int32 [4, 1536], P('visit', 'patch'), may hold values from 0 to 15
- coeff_table: float32 [16, 3], replicated, may hold values from -4 to 4
- basis_taps: float32 [3, 2, 21], replicated, may hold values from -1.25 to 1.25
Outputs:
- coadd: float32 [64, 256, 256], P('patch', 'visit')
The draws below stay inside these ranges and needn't reach their ends.
Inputs may be any that keep to these rules, and one draw needn't show every extreme that they name: Each row names 2 different patches; in the rows of one device no patch is named more than 2 times, a bound that some block reaches. `variance`: positive.
All inputs are finite; a program needn't handle non-finite values.
Results may differ from the reference program's by a relative error of at most 0.00014.
Values sent between devices are 32-bit elements; how exact they have to be, the bound alone decides.
No kernel may reach another device: no remote copies, remote signals or barrier semaphores. Data moves between devices by JAX's collectives and lax.ppermute only.
A program may use at most 64 MiB of HBM per device.

```python
import math
import jax
import jax.numpy as jnp
import numpy as np
from jax import lax

TILE_PIX = 128
PATCH_PIX = 256
TAPS = 21
NB = 3
NCOEF = 16
TOP = 2
TILE_DEV = 24
TILES_V = 1536
NPATCH = 64
CAP = 2
N_VISIT = 4


def draw_variance(key, part):
    key = jax.random.fold_in(key, 11)
    key_tile, key_rows, key_cols, key_noise = jax.random.split(key, 4)
    tile_low, tile_high, noise_low, noise_high = (0.1, 10.0, 0.5, 1.5)
    tile_scale = jnp.exp(jax.random.uniform(key_tile, (N_VISIT, TILES_V, 1, 1), jnp.float32, math.log(tile_low), math.log(tile_high)))
    row_scale = jnp.exp(jax.random.uniform(key_rows, (N_VISIT, TILES_V, TILE_PIX, 1), jnp.float32, 0.0, math.log(10.0)))
    col_scale = jnp.exp(jax.random.uniform(key_cols, (N_VISIT, TILES_V, 1, TILE_PIX), jnp.float32, 0.0, math.log(10.0)))
    noise = jax.random.uniform(key_noise, (N_VISIT, TILES_V, TILE_PIX, TILE_PIX), jnp.float32, noise_low, noise_high)
    return (tile_scale * row_scale * col_scale * noise).astype(jnp.float32)


def with_ends(array, rng, least, high):
    dims = array.shape
    place = [jax.random.randint(jax.random.fold_in(rng, axis), (), 0, dims[axis]) for axis in range(len(dims))]
    array = array.at[tuple(place)].set(least)
    longest = dims.index(max(dims))
    place[longest] = (place[longest] + 1) % dims[longest]
    return array.at[tuple(place)].set(high)


def steps_of(stream_key, extent, cuts, least, largest):
    factor_of = 1.0
    for position, parts in cuts:
        draws = jax.random.uniform(jax.random.fold_in(jax.random.fold_in(stream_key, 6), position), (parts,), jnp.float32, least / len(cuts), largest / len(cuts))
        factor_of = factor_of * jnp.repeat(jnp.exp(draws), extent[position] // parts).reshape((-1,) + (1,) * (len(extent) - 1 - position))
    return factor_of


def assign_block(rng, own, number, rows, number_of, top, most, lean):
    ranking = jax.random.permutation(rng, number_of)
    heavy_load, common = portions_of(number_of, rows * top, most, lean, True), portions_of(number_of, rows * top, most, lean, False)
    places = jnp.arange(number_of)

    def named(lengths, offset_by):
        used = int((lengths > 0).sum())
        fixed = max(1, used // 4)
        moved = fixed + (places - fixed + offset_by * (used - fixed)) % max(1, number_of - fixed)
        return jnp.zeros((number_of,), jnp.int32).at[ranking[jnp.where(places < fixed, places, moved)]].set(jnp.asarray(lengths, jnp.int32))

    lengths = jnp.where(number % 4 == 0, named(heavy_load, number // 4), named(common, number - number // 4 - 1))
    mixed = jax.random.permutation(jax.random.fold_in(own, 3), number_of)
    donor, taker = mixed[0:number_of // 2 * 2:2], mixed[1:number_of // 2 * 2:2]
    room = jnp.minimum(lengths[donor] - 1, most - lengths[taker]) // 2
    room = jnp.where((donor == ranking[0]) | (taker == ranking[0]) | (lengths[taker] == 0), 0, jnp.maximum(room, 0))
    moved = jax.random.randint(jax.random.fold_in(own, 4), (number_of // 2,), 0, 1 << 20) % (room + 1)
    lengths = lengths.at[donor].add(-moved).at[taker].add(moved)
    members = jnp.searchsorted(jnp.cumsum(lengths), jnp.arange(rows * top), side="right").astype(jnp.int32)
    grid = members.reshape(top, rows).T
    grid = grid[jax.random.permutation(jax.random.fold_in(own, 1), rows)]
    offset_by = jax.random.randint(jax.random.fold_in(own, 2), (rows, 1), 0, top)
    return jnp.take_along_axis(grid, (jnp.arange(top)[None, :] + offset_by) % top, axis=1)


def portions_of(amount, total, bound, lean, full):
    weights = [(1 << 20) // math.isqrt(rank ** lean) + 1 for rank in range(1, amount + 1)]
    largest = bound if full else min(bound, max(-(-total // amount), total * weights[0] // sum(weights)))
    least = 1 if total - largest >= amount - 1 else 0
    holding, rest = [largest] + [least] * (amount - 1), total - largest - least * (amount - 1)
    while rest > 0:
        movable = [i for i in range(1, amount) if holding[i] < largest] or [i for i in range(1, amount) if holding[i] < bound]
        mass, budget = sum([weights[i] for i in movable]), rest
        for i in movable:
            extra = min(bound - holding[i], max(1, budget * weights[i] // mass), rest)
            holding[i] = holding[i] + extra
            rest = rest - extra
    return np.array(holding)


def bell_draw(rng, extent, scale, limit, cuts=(), kind=jnp.bfloat16):
    gain = steps_of(rng, extent, cuts, -0.22, 0.18) if cuts else 1.0
    drawn = jax.random.normal(rng, extent, jnp.float32) * scale * gain
    return jnp.minimum(jnp.maximum(drawn, -limit), limit).astype(kind)


def setup_inputs(seed: int = 0) -> dict:
    keys = jax.random.split(jax.random.key(seed), 8)
    image = bell_draw(keys[0], (N_VISIT, TILES_V, TILE_PIX, TILE_PIX), 1.0, 6.0, ((0, 4), (1, 64)), jnp.float32)
    variance = draw_variance(jax.random.fold_in(keys[7], 71), 0)
    patches_keys = jax.random.split(jax.random.fold_in(keys[2], 1), N_VISIT * TILES_V // TILE_DEV)
    patches_turns = jax.random.permutation(jax.random.fold_in(keys[2], 3), N_VISIT * TILES_V // TILE_DEV)
    patches = jax.vmap(lambda own, number: assign_block(jax.random.fold_in(keys[2], 2), own, number, TILE_DEV, NPATCH, TOP, CAP, 2))(patches_keys, patches_turns).reshape((N_VISIT, TILES_V, TOP))
    offsets = with_ends(jax.random.randint(keys[3], (N_VISIT, TILES_V, TOP, 2), -(TILE_PIX // 2), PATCH_PIX - TILE_PIX // 2 + 1), jax.random.fold_in(keys[3], 1), -(TILE_PIX // 2), (PATCH_PIX - TILE_PIX // 2 + 1) - 1).astype(jnp.int32)
    psf_index = with_ends(jax.random.randint(keys[4], (N_VISIT, TILES_V), 0, NCOEF), jax.random.fold_in(keys[4], 1), 0, NCOEF - 1).astype(jnp.int32)
    coeff_table = bell_draw(keys[5], (NCOEF, NB), 1.0, 4.0, (), jnp.float32)
    basis_taps = bell_draw(keys[6], (NB, 2, TAPS), TAPS ** -0.5, 1.25, (), jnp.float32)
    return dict(image=image, variance=variance, patches=patches, offsets=offsets, psf_index=psf_index, coeff_table=coeff_table, basis_taps=basis_taps)


def blur_tiles(tile_stack, coeffs, basis_taps):
    pixels = tile_stack.shape[-1]
    tap_count = basis_taps.shape[-1]
    margin = tap_count // 2
    padded = jnp.pad(tile_stack, ((0, 0), (margin, margin), (margin, margin)))
    result = jnp.zeros(tile_stack.shape, jnp.float32)
    for basis_idx in range(basis_taps.shape[0]):
        rowwise = jnp.zeros((tile_stack.shape[0], pixels, pixels + 2 * margin), jnp.float32)
        for shift_u in range(tap_count):
            rowwise = rowwise + basis_taps[basis_idx, 0, shift_u] * padded[:, shift_u:shift_u + pixels, :]
        both_ways = jnp.zeros(tile_stack.shape, jnp.float32)
        for shift_v in range(tap_count):
            both_ways = both_ways + basis_taps[basis_idx, 1, shift_v] * rowwise[:, :, shift_v:shift_v + pixels]
        result = result + coeffs[:, basis_idx, None, None] * both_ways
    return result


def reference(image, variance, patches, offsets, psf_index, coeff_table, basis_taps):
    tile_count = N_VISIT * TILES_V
    tile_stack = image.reshape(tile_count, TILE_PIX, TILE_PIX)
    weights = 1.0 / jnp.mean(variance.reshape(tile_count, TILE_PIX * TILE_PIX), axis=1)
    coeffs = coeff_table[psf_index.reshape(tile_count).astype(jnp.int32)]
    group_size = math.gcd(tile_count, 64)
    blurred = lax.map(
        lambda payload: blur_tiles(payload[0], payload[1], basis_taps),
        (tile_stack.reshape(tile_count // group_size, group_size, TILE_PIX, TILE_PIX),
         coeffs.reshape(tile_count // group_size, group_size, NB)),
    ).reshape(tile_count, TILE_PIX, TILE_PIX)
    weighted = weights[:, None, None] * blurred
    targets = patches.reshape(-1).astype(jnp.int32)
    owners = (jnp.arange(tile_count * TOP, dtype=jnp.int32) // TOP).astype(jnp.int32)
    shifts = offsets.reshape(-1, 2).astype(jnp.int32) + TILE_PIX // 2
    unit_tile = jnp.ones((1, TILE_PIX, TILE_PIX), jnp.float32)

    def advance(running, element):
        numerator, denominator = running
        target, source, shift_row, shift_col = element
        corner = (target, shift_row, shift_col)
        current = lax.dynamic_slice(numerator, corner, (1, TILE_PIX, TILE_PIX))
        numerator = lax.dynamic_update_slice(numerator, current + weighted[source][None], corner)
        covered = lax.dynamic_slice(denominator, corner, (1, TILE_PIX, TILE_PIX))
        denominator = lax.dynamic_update_slice(denominator, covered + weights[source] * unit_tile, corner)
        return (numerator, denominator), None

    width = PATCH_PIX + TILE_PIX
    zero_sums = (jnp.zeros((NPATCH, width, width), jnp.float32), jnp.zeros((NPATCH, width, width), jnp.float32))
    (numerator, denominator), unused = lax.scan(advance, zero_sums, (targets, owners, shifts[:, 0], shifts[:, 1]))
    low = TILE_PIX // 2
    numerator = numerator[:, low:low + PATCH_PIX, low:low + PATCH_PIX]
    denominator = denominator[:, low:low + PATCH_PIX, low:low + PATCH_PIX]
    return numerator / (denominator + 1.0)
```

```python
import functools

import jax
import jax.numpy as jnp
from jax import lax
from jax.experimental import pallas as pl
from jax.experimental.pallas import tpu as pltpu
from jax.sharding import Mesh
from jax.sharding import PartitionSpec as P

PIX = 128
PATCH_PIX = 256
TAPS = 21
MARGIN = TAPS // 2
NB = 3
NX, NZ, NC, NY = 4, 8, 2, 4
STRIP = PATCH_PIX // NY
HALF = 12
F32 = jnp.float32
BF16 = jnp.bfloat16
VMEM_LIMIT = 40 * 1024 * 1024


def split(value):
    high = value.astype(BF16)
    return high, (value - high.astype(F32)).astype(BF16)


def dot(a, b):
    return jnp.dot(a, b, preferred_element_type=F32)


def blur_kernel(first, psf_ref, table_ref, taps_ref, img_ref, var_ref, out_ref, wts_ref,
                col_hi, col_lo, row_hi, row_lo):
    major = lax.broadcasted_iota(jnp.int32, (PIX, PIX), 0)
    minor = lax.broadcasted_iota(jnp.int32, (PIX, PIX), 1)
    for b in range(NB):
        for axis, diff in ((0, minor - major), (1, major - minor)):
            band = jnp.zeros((PIX, PIX), F32)
            for t in range(TAPS):
                band = jnp.where(diff == t - MARGIN, taps_ref[2 * b + axis, t], band)
            hi, lo = split(band)
            place = (slice(None), slice(b * PIX, (b + 1) * PIX))
            if axis:
                col_hi[place], col_lo[place] = hi, lo
            else:
                row_hi[place], row_lo[place] = hi, lo
    for pair in range(HALF // 2):
        x_hi, x_lo = split(img_ref[0, 2 * pair:2 * pair + 2].reshape(2 * PIX, PIX))
        smooth = dot(x_hi, col_hi[...]) + (dot(x_lo, col_hi[...]) + dot(x_hi, col_lo[...]))
        sides = []
        for n in range(2):
            tile = 2 * pair + n
            total = jnp.sum(jnp.sum(var_ref[0, tile], axis=0, keepdims=True), axis=1, keepdims=True)
            weight = 1.0 / (total * (1.0 / (PIX * PIX)))
            wts_ref[tile:tile + 1, :] = jnp.broadcast_to(weight, (1, PIX))
            row = psf_ref[0, first + tile]
            sides.append(jnp.concatenate(
                [smooth[n * PIX:(n + 1) * PIX, b * PIX:(b + 1) * PIX] * (table_ref[row, b] * weight)
                 for b in range(NB)], axis=0))
        q_hi, q_lo = split(jnp.concatenate(sides, axis=1))
        done = dot(row_hi[...], q_hi) + (dot(row_hi[...], q_lo) + dot(row_lo[...], q_hi))
        for n in range(2):
            tile = 2 * pair + n
            out_ref[tile * PIX:(tile + 1) * PIX, :] = done[:, n * PIX:(n + 1) * PIX]


def blur_half(half, psf_index, coeff_table, taps, image, variance):
    smem = pl.BlockSpec(memory_space=pltpu.SMEM)
    tiles = pl.BlockSpec((1, HALF, PIX, PIX), lambda i: (0, half, 0, 0))
    return pl.pallas_call(
        functools.partial(blur_kernel, half * HALF),
        grid=(1,),
        in_specs=[smem, smem, smem, tiles, tiles],
        out_specs=[pl.BlockSpec((HALF * PIX, PIX), lambda i: (0, 0)),
                   pl.BlockSpec((HALF, PIX), lambda i: (0, 0))],
        out_shape=[jax.ShapeDtypeStruct((HALF * PIX, PIX), F32),
                   jax.ShapeDtypeStruct((HALF, PIX), F32)],
        scratch_shapes=[pltpu.VMEM((PIX, NB * PIX), BF16)] * 4,
        compiler_params=pltpu.CompilerParams(vmem_limit_bytes=VMEM_LIMIT),
        cost_estimate=pl.CostEstimate(flops=HALF * 76 * 10**6, bytes_accessed=HALF * 3 * 65536,
                                      transcendentals=0),
        name="blur_half",
    )(psf_index, coeff_table, taps, image, variance)


def place_kernel(fresh, firsts, here_ref, meta_a, meta_b, tiles_a, tiles_b, *refs):
    if fresh:
        mine, theirs, buf, sems = refs
        mine[...] = jnp.zeros(mine.shape, F32)
        theirs[...] = jnp.zeros(theirs.shape, F32)
    else:
        old_mine, old_theirs, mine, theirs, buf, sems = refs
    copies = []
    for n, source in enumerate((tiles_a, tiles_b)):
        copies.append(pltpu.make_async_copy(
            source, buf.at[pl.ds(STRIP + n * HALF * PIX, HALF * PIX)], sems.at[n]))
        copies[-1].start()
    buf[0:STRIP] = jnp.zeros((STRIP, PIX), F32)
    buf[STRIP + 2 * HALF * PIX:] = jnp.zeros((STRIP, PIX), F32)
    if not fresh:
        mine[...] = old_mine[...]
        theirs[...] = old_theirs[...]
    core, strip = here_ref[0], here_ref[1]
    row_of = lax.broadcasted_iota(jnp.int32, (STRIP, PIX), 0)
    lane = lax.broadcasted_iota(jnp.int32, (STRIP, PIX), 1)
    for copy in copies:
        copy.wait()

    def add(canvas, patch, tile_row, skip, col):
        rows = buf[pl.ds(tile_row + skip, STRIP), :]
        rows = pltpu.roll(rows, (col + PIX) & (PIX - 1), 1)
        line = row_of + skip
        inside = (line >= 0) & (line < PIX)
        for side in range(2):
            pixel = lane + (side * PIX - col)
            hit = inside & (pixel >= 0) & (pixel < PIX)
            canvas[patch, side] += jnp.where(hit, rows, 0.0)

    for n, meta in enumerate((meta_a, meta_b)):
        def step(t, carry, n=n, meta=meta):
            for k in range(2):
                at = 6 * (firsts[n] + t) + 3 * k
                patch, row, col = meta[at], meta[at + 1], meta[at + 2]
                skip = strip * STRIP - row
                tile_row = STRIP + (n * HALF + t) * PIX
                touched = (skip > -STRIP) & (skip < PIX)
                own = (patch & 1) == core

                @pl.when(touched & own)
                def _():
                    add(mine, patch >> 1, tile_row, skip, col)

                @pl.when(touched & jnp.logical_not(own))
                def _():
                    add(theirs, patch >> 1, tile_row, skip, col)
            return carry

        lax.fori_loop(0, HALF, step, 0)


def place(here, metas, firsts, tiles, canvas):
    smem = pl.BlockSpec(memory_space=pltpu.SMEM)
    hbm = pl.BlockSpec(memory_space=pl.ANY)
    vmem = pl.BlockSpec(memory_space=pltpu.VMEM)
    shape = jax.ShapeDtypeStruct((NX * NZ, 2, STRIP, PIX), F32)
    fresh = canvas is None
    return pl.pallas_call(
        functools.partial(place_kernel, fresh, firsts),
        in_specs=[smem] * 3 + [hbm] * 2 + ([] if fresh else [vmem] * 2),
        out_specs=[vmem] * 2,
        out_shape=[shape] * 2,
        scratch_shapes=[pltpu.VMEM((2 * STRIP + 2 * HALF * PIX, PIX), F32),
                        pltpu.SemaphoreType.DMA((2,))],
        compiler_params=pltpu.CompilerParams(vmem_limit_bytes=VMEM_LIMIT),
        cost_estimate=pl.CostEstimate(flops=20 * 10**6, bytes_accessed=10 * 10**6, transcendentals=0),
        name="place",
    )(here, *metas, *tiles, *(() if fresh else canvas))


def shift(value, axis, by):
    size = lax.axis_size(axis)
    return lax.ppermute(value, axis, [(i, (i + by) % size) for i in range(size)])


def weight_sums(weights, patches, offsets, strip):
    tile_dev = weights.shape[0]
    npatch = NX * NZ * NC
    pairs = tile_dev * 2
    targets = patches.reshape(pairs)
    matches = (targets[:, None] == jnp.arange(npatch, dtype=jnp.int32)[None, :]).astype(jnp.int32)
    earlier = jnp.sum((jnp.cumsum(matches, axis=0) - matches) * matches, axis=1)
    slot_of = targets * 2 + earlier
    chooser = (jnp.arange(npatch * 2, dtype=jnp.int32)[:, None] == slot_of[None, :]).astype(F32)
    payload = jnp.concatenate(
        [jnp.repeat(weights, 2)[:, None], offsets.reshape(pairs, 2).astype(F32)], axis=1)
    sent = jnp.dot(chooser, payload, precision=lax.Precision.HIGHEST).reshape(npatch, 6)
    got = lax.all_to_all(sent, ("x", "z", "core"), 0, 0, tiled=True)
    every = jnp.stack([got] + [shift(got, "y", k) for k in (1, 2, 3)]).reshape(-1, 3)
    rows = strip * STRIP + jnp.arange(STRIP, dtype=jnp.int32)
    cols = jnp.arange(PATCH_PIX, dtype=jnp.int32)
    row_at = rows[None, :] - every[:, 1:2].astype(jnp.int32)
    col_at = cols[None, :] - every[:, 2:3].astype(jnp.int32)
    row_hit = ((row_at >= 0) & (row_at < PIX)).astype(F32) * every[:, 0:1]
    col_hit = ((col_at >= 0) & (col_at < PIX)).astype(F32)
    return jnp.einsum("na,nb->ab", row_hit, col_hit, precision=lax.Precision.HIGHEST)


def body(image, variance, patches, offsets, psf_index, coeff_table, basis_taps):
    strip = lax.axis_index("y")
    here = jnp.stack([lax.axis_index("core"), strip]).astype(jnp.int32)
    taps = basis_taps.reshape(NB * 2, TAPS)
    meta = jnp.concatenate([patches[0][..., None], offsets[0]], axis=-1).reshape(-1)
    own_a, wts_a = blur_half(0, psf_index, coeff_table, taps, image, variance)
    own_b, wts_b = blur_half(1, psf_index, coeff_table, taps, image, variance)

    meta_left, meta_right, meta_far = (shift(meta, "y", k) for k in (1, -1, 2))
    left_a = shift(own_a, "y", 1)
    right_b = shift(own_b, "y", -1)
    left_a, right_b, next_a, next_b = lax.optimization_barrier((left_a, right_b, own_a, own_b))
    far_a = shift(left_a, "y", 1)
    far_b = shift(right_b, "y", -1)
    left_b = shift(next_b, "y", 1)
    right_a = shift(next_a, "y", -1)

    canvas = place(here, (meta, meta), (0, HALF), (own_a, own_b), None)
    canvas = place(here, (meta_left, meta_right), (0, HALF), (left_a, right_b), canvas)
    canvas = place(here, (meta_left, meta_right), (HALF, 0), (left_b, right_a), canvas)
    mine, theirs = place(here, (meta_far, meta_far), (0, HALF), (far_a, far_b), canvas)

    weights = jnp.concatenate([wts_a[:, 0], wts_b[:, 0]])
    denominator = weight_sums(weights, patches, offsets, strip)

    partial = mine + shift(theirs, "core", 1)
    partial = partial.reshape(NX, NZ * 2 * STRIP, PIX)
    partial = lax.all_to_all(partial, "x", 0, 0, tiled=True).sum(axis=0)
    partial = partial.reshape(NZ, 2 * STRIP, PIX)
    total = lax.all_to_all(partial, "z", 0, 0, tiled=True).sum(axis=0)
    numerator = jnp.concatenate([total[:STRIP], total[STRIP:]], axis=1)
    return (numerator / (denominator + 1.0))[None]


def solution(mesh):
    fine = Mesh(mesh.devices.reshape(NX, NZ, NC, NY), ("x", "z", "core", "y"))
    own = ("x", "z", "core")
    return jax.shard_map(
        body,
        mesh=fine,
        in_specs=(
            P("y", own, None, None),
            P("y", own, None, None),
            P("y", own, None),
            P("y", own, None, None),
            P("y", own),
            P(),
            P(),
        ),
        out_specs=P(own, "y", None),
        check_vma=False,
    )
```

```python
import functools

import jax
import jax.numpy as jnp
from jax import lax
from jax.experimental import pallas as pl
from jax.experimental.pallas import tpu as pltpu
from jax.sharding import Mesh
from jax.sharding import PartitionSpec as P

PIX = 128
PATCH_PIX = 256
TAPS = 21
MARGIN = TAPS // 2
NB = 3
NX, NZ, NC, NY = 4, 8, 2, 4
STRIP = PATCH_PIX // NY
HALF = 12
STEP = 6
UNROLL = 3
META = 8
F32 = jnp.float32
BF16 = jnp.bfloat16
BLUR_LIMIT = 56 * 1024 * 1024
PLACE_LIMIT = 24 * 1024 * 1024
ADD_LIMIT = 8 * 1024 * 1024


def split(value):
    high = value.astype(BF16)
    return high, (value - high.astype(F32)).astype(BF16)


def dot(a, b):
    return jnp.dot(a, b, preferred_element_type=F32)


def blur_kernel(first, psf_ref, table_ref, taps_ref, patch_ref, offset_ref, img_ref, var_ref, out_ref, wts_ref,
                col_hi, col_lo, row_hi, row_lo):
    now = pl.program_id(0)

    @pl.when(now == 0)
    def _():
        major = lax.broadcasted_iota(jnp.int32, (PIX, PIX), 0)
        minor = lax.broadcasted_iota(jnp.int32, (PIX, PIX), 1)
        for b in range(NB):
            for axis, diff in ((0, minor - major), (1, major - minor)):
                band = jnp.zeros((PIX, PIX), F32)
                for t in range(TAPS):
                    band = jnp.where(diff == t - MARGIN, taps_ref[b, axis, t], band)
                hi, lo = split(band)
                place = (slice(None), slice(b * PIX, (b + 1) * PIX))
                if axis:
                    col_hi[place], col_lo[place] = hi, lo
                else:
                    row_hi[place], row_lo[place] = hi, lo
        lane = lax.broadcasted_iota(jnp.int32, (META, PIX), 1)
        facts = jnp.zeros((META, PIX), jnp.int32)
        for n in range(HALF):
            for k in range(2):
                values = (patch_ref[0, k, first + n], offset_ref[0, k, 0, first + n], offset_ref[0, k, 1, first + n])
                for m, value in enumerate(values):
                    facts = jnp.where(lane == 6 * n + 3 * k + m, value, facts)
        out_ref[0:META, :] = facts.astype(F32)

    for pair in range(STEP // 2):
        x_hi, x_lo = split(img_ref[0, 2 * pair:2 * pair + 2].reshape(2 * PIX, PIX))
        smooth = dot(x_hi, col_hi[...]) + (dot(x_lo, col_hi[...]) + dot(x_hi, col_lo[...]))
        sides = []
        for n in range(2):
            tile = now * STEP + 2 * pair + n
            total = jnp.sum(jnp.sum(var_ref[0, 2 * pair + n], axis=0, keepdims=True), axis=1, keepdims=True)
            weight = 1.0 / (total * (1.0 / (PIX * PIX)))
            wts_ref[pl.ds(tile, 1), :] = jnp.broadcast_to(weight, (1, PIX))
            row = psf_ref[0, first + tile]
            sides.append(jnp.concatenate(
                [smooth[n * PIX:(n + 1) * PIX, b * PIX:(b + 1) * PIX] * (table_ref[b, row] * weight)
                 for b in range(NB)], axis=0))
        q_hi, q_lo = split(jnp.concatenate(sides, axis=1))
        done = dot(row_hi[...], q_hi) + (dot(row_hi[...], q_lo) + dot(row_lo[...], q_hi))
        for n in range(2):
            tile = now * STEP + 2 * pair + n
            out_ref[pl.ds(META + tile * PIX, PIX), :] = done[:, n * PIX:(n + 1) * PIX]


def blur_half(half, psf_index, table, taps, patches, offsets, image, variance):
    smem = pl.BlockSpec(memory_space=pltpu.SMEM)
    tiles = pl.BlockSpec((1, STEP, PIX, PIX), lambda i: (0, half * HALF // STEP + i, 0, 0))
    rows = META + HALF * PIX
    return pl.pallas_call(
        functools.partial(blur_kernel, half * HALF),
        grid=(HALF // STEP,),
        in_specs=[smem] * 5 + [tiles, tiles],
        out_specs=[pl.BlockSpec((rows, PIX), lambda i: (0, 0)),
                   pl.BlockSpec((HALF, PIX), lambda i: (0, 0))],
        out_shape=[jax.ShapeDtypeStruct((rows, PIX), F32),
                   jax.ShapeDtypeStruct((HALF, PIX), F32)],
        scratch_shapes=[pltpu.VMEM((PIX, NB * PIX), BF16)] * 4,
        compiler_params=pltpu.CompilerParams(vmem_limit_bytes=BLUR_LIMIT),
        cost_estimate=pl.CostEstimate(flops=HALF * 76 * 10**6, bytes_accessed=HALF * 3 * 65536,
                                      transcendentals=0),
        name="blur_half",
    )(psf_index, table, taps, patches, offsets, image, variance)


def halves_kernel(*refs):
    for n in range(4):
        rows = refs[4 + n].shape[0] - META
        start = META if n % 2 == 0 else META + rows
        refs[4 + n][0:META] = refs[n][0:META]
        refs[4 + n][META:] = refs[n][start:start + rows]


def halves(*arrays):
    vmem = pl.BlockSpec(memory_space=pltpu.VMEM)
    rows = META + HALF * PIX // 2
    return pl.pallas_call(
        halves_kernel,
        in_specs=[vmem] * 4,
        out_specs=[vmem] * 4,
        out_shape=[jax.ShapeDtypeStruct((rows, PIX), F32)] * 4,
        compiler_params=pltpu.CompilerParams(vmem_limit_bytes=ADD_LIMIT),
        name="halves",
    )(*arrays)


def place_kernel(runs, olds, both, last, here_ref, *refs):
    count = len(runs)
    tiles, old, refs = refs[:count], refs[count:count + olds], refs[count + olds:]
    outs, (canvas, buf, facts, meta_ref, sems) = refs[:10], refs[-5:]
    copies, starts, at = [], [], STRIP
    for n, source in enumerate(tiles):
        copies.append(pltpu.make_async_copy(source, buf.at[pl.ds(at, source.shape[0])], sems.at[n]))
        copies[-1].start()
        buf[at - STRIP:at] = jnp.zeros((STRIP, PIX), F32)
        starts.append(at + META)
        at += source.shape[0] + STRIP
    buf[at - STRIP:at] = jnp.zeros((STRIP, PIX), F32)
    if old:
        canvas[...] = old[0][...] + old[1][...] if len(old) > 1 else old[0][...]
    else:
        canvas[...] = jnp.zeros(canvas.shape, F32)
    my_x, core, my_y = here_ref[0], here_ref[1], here_ref[2]
    for n, copy in enumerate(copies):
        copy.wait()
        facts[n * META:(n + 1) * META] = buf[starts[n] - META:starts[n]].astype(jnp.int32)
    to_scalars = pltpu.make_async_copy(facts, meta_ref, sems.at[count])
    to_scalars.start()
    to_scalars.wait()
    row_of = lax.broadcasted_iota(jnp.int32, (8, PIX), 0)
    lane = lax.broadcasted_iota(jnp.int32, (8, PIX), 1)

    def add(items):
        moved = [pltpu.roll(buf[pl.ds(tile_row + skip, STRIP), :], (col + PIX) & (PIX - 1), 1)
                 for _, tile_row, skip, col in items]
        for (at, _, skip, col), strip in zip(items, moved):
            sides = [(lane >= col - n * PIX) & (lane < col - n * PIX + PIX) for n in range(2)]
            for g in range(0, STRIP, 8):
                line = row_of + (skip + g)
                inside = (line >= 0) & (line < PIX)
                for n in range(2):
                    canvas[at, n, g:g + 8] += jnp.where(inside & sides[n], strip[g:g + 8], 0.0)

    def bounded(skip):
        return jnp.clip(skip, -STRIP, PIX)

    def pair_of(index, entry):
        patch, row, col = (meta_ref[index * META, entry + n] for n in range(3))
        return patch, (patch >> 1) & (NZ - 1), patch >> 4, row, col

    def along_y(t, carry, index, entry, base):
        items = []
        for n in range(UNROLL):
            for k in range(2):
                patch, column, owner, row, col = pair_of(index, entry + 6 * (UNROLL * t + n) + 3 * k)
                at = ((owner - my_x) & (NX - 1)) * NZ + column
                skip = bounded(my_y * STRIP - row)
                other = (patch & 1) != core
                if both:
                    at = at + jnp.where(other, 2 * NX * NZ, 0)
                else:
                    skip = jnp.where(other, PIX, skip)
                items.append((at, base + (UNROLL * t + n) * PIX, skip, col))
        add(items)
        return carry

    def along_x(t, carry, index, entry, base):
        for k in range(2):
            patch, column, owner, row, col = pair_of(index, entry + 6 * t + 3 * k)
            other = (patch & 1) != core
            top = jnp.maximum(row, 0) // STRIP

            @pl.when((owner == my_x) if both else (owner == my_x) & jnp.logical_not(other))
            def _():
                items = []
                for n in range(3):
                    strip = top + n
                    skip = jnp.where(strip < NY, bounded(strip * STRIP - row), PIX)
                    at = (NX + ((strip - my_y) & (NY - 1))) * NZ + column
                    if both:
                        at = at + jnp.where(other, 2 * NX * NZ, 0)
                    items.append((at, base + t * PIX, skip, col))
                add(items)
        return carry

    for index, (group, tile, size) in enumerate(runs):
        given = dict(index=index, entry=6 * tile, base=starts[index])
        if group == 0:
            lax.fori_loop(0, size // UNROLL, functools.partial(along_y, **given), 0)
        else:
            lax.fori_loop(0, size, functools.partial(along_x, **given), 0)
    if last:
        half = NZ // 2
        for group in range(2):
            own, right, far, left = (group * NX * NZ + n * NZ for n in range(4))
            to_right, to_left, right_low, left_high, stay = outs[5 * group:5 * group + 5]
            to_right[:half] = canvas[far:far + half]
            to_right[half:] = canvas[right + half:right + NZ]
            to_left[:half] = canvas[far + half:far + NZ]
            to_left[half:] = canvas[left:left + half]
            right_low[...] = canvas[right:right + half]
            left_high[...] = canvas[left + half:left + NZ]
            stay[...] = canvas[own:own + NZ]
    elif both:
        refs[0][...] = canvas[:2 * NX * NZ]
        refs[1][...] = canvas[2 * NX * NZ:]
    else:
        refs[0][...] = canvas[...]


def place(here, arrays, old=(), both=False, last=False, cost=4):
    smem = pl.BlockSpec(memory_space=pltpu.SMEM)
    hbm = pl.BlockSpec(memory_space=pl.ANY)
    vmem = pl.BlockSpec(memory_space=pltpu.VMEM)
    size = 2 * NX * NZ
    shape = jax.ShapeDtypeStruct((size, 2, STRIP, PIX), F32)
    whole = jax.ShapeDtypeStruct((NZ, 2, STRIP, PIX), F32)
    half = jax.ShapeDtypeStruct((NZ // 2, 2, STRIP, PIX), F32)
    count = len(arrays)
    rows = sum(a.shape[0] + STRIP for _, _, a in arrays) + STRIP
    runs = tuple((group, tile, a.shape[0] // PIX) for group, tile, a in arrays)
    outs = [whole, whole, half, half, whole] * 2 if last else [shape] * (2 if both else 1)
    return pl.pallas_call(
        functools.partial(place_kernel, runs, len(old), both, last),
        in_specs=[smem] + [hbm] * count + [vmem] * len(old),
        out_specs=[vmem] * len(outs),
        out_shape=outs,
        scratch_shapes=[pltpu.VMEM((size * (2 if both else 1), 2, STRIP, PIX), F32),
                        pltpu.VMEM((rows, PIX), F32),
                        pltpu.VMEM((count * META, PIX), jnp.int32),
                        pltpu.SMEM((count * META, PIX), jnp.int32),
                        pltpu.SemaphoreType.DMA((count + 1,))],
        compiler_params=pltpu.CompilerParams(vmem_limit_bytes=PLACE_LIMIT),
        cost_estimate=pl.CostEstimate(flops=10**6, bytes_accessed=cost * 3690000, transcendentals=0),
        name="place",
    )(here, *(a for _, _, a in arrays), *old)


def add_kernel(*refs):
    number = len(refs) // 3
    for n in range(number):
        refs[2 * number + n][...] = refs[n][...] + refs[number + n][0:refs[n].shape[0]]


def add_received(mine, received):
    vmem = pl.BlockSpec(memory_space=pltpu.VMEM)
    return pl.pallas_call(
        add_kernel,
        in_specs=[vmem] * (2 * len(mine)),
        out_specs=[vmem] * len(mine),
        out_shape=[jax.ShapeDtypeStruct(a.shape, F32) for a in mine],
        compiler_params=pltpu.CompilerParams(vmem_limit_bytes=ADD_LIMIT),
        name="add_received",
    )(*mine, *received)


def join_kernel(stay_a, stay_b, *refs):
    out = refs[-1]
    half = NZ // 2
    low = stay_a[:half] + stay_b[:half]
    high = stay_a[half:] + stay_b[half:]
    for from_left, from_right, left_last, right_last in (refs[0:4], refs[4:8]):
        low = low + (from_right[half:] + left_last[...])
        high = high + (from_left[half:] + right_last[...])
    out[:half] = low
    out[half:] = high


def join(stay_a, stay_b, *received):
    vmem = pl.BlockSpec(memory_space=pltpu.VMEM)
    return pl.pallas_call(
        join_kernel,
        in_specs=[vmem] * 10,
        out_specs=vmem,
        out_shape=jax.ShapeDtypeStruct(stay_a.shape, F32),
        compiler_params=pltpu.CompilerParams(vmem_limit_bytes=ADD_LIMIT),
        name="join",
    )(stay_a, stay_b, *received)


def shift(value, axis, by):
    size = lax.axis_size(axis)
    return lax.ppermute(value, axis, [(i, (i + by) % size) for i in range(size)])


def pairs_of_patch(weights, patches, offsets):
    tile_dev = weights.shape[0]
    npatch = NX * NZ * NC
    pairs = tile_dev * 2
    targets = patches.reshape(pairs)
    matches = (targets[:, None] == jnp.arange(npatch, dtype=jnp.int32)[None, :]).astype(jnp.int32)
    earlier = jnp.sum((jnp.cumsum(matches, axis=0) - matches) * matches, axis=1)
    slot_of = targets * 2 + earlier
    chooser = (jnp.arange(npatch * 2, dtype=jnp.int32)[:, None] == slot_of[None, :]).astype(F32)
    payload = jnp.concatenate(
        [jnp.repeat(weights, 2)[:, None], offsets.reshape(pairs, 2).astype(F32)], axis=1)
    sent = jnp.dot(chooser, payload, precision=lax.Precision.HIGHEST).reshape(NX, NZ, NC, 1, 6)
    sent = jnp.broadcast_to(sent, (NX, NZ, NC, NY, 6)).reshape(-1, 6)
    return lax.all_to_all(sent, ("x", "z", "core", "y"), 0, 0, tiled=True)


def weight_sums(got, strip):
    every = got.reshape(-1, 3)
    rows = strip * STRIP + jnp.arange(STRIP, dtype=jnp.int32)
    cols = jnp.arange(PATCH_PIX, dtype=jnp.int32)
    row_at = rows[None, :] - every[:, 1:2].astype(jnp.int32)
    col_at = cols[None, :] - every[:, 2:3].astype(jnp.int32)
    row_hit = ((row_at >= 0) & (row_at < PIX)).astype(F32) * every[:, 0:1]
    col_hit = ((col_at >= 0) & (col_at < PIX)).astype(F32)
    return jnp.einsum("na,nb->ab", row_hit, col_hit, precision=lax.Precision.HIGHEST)


def body(image, variance, patches, offsets, psf_index, coeff_table, basis_taps):
    strip = lax.axis_index("y")
    here = jnp.stack([lax.axis_index("x"), lax.axis_index("core"), strip]).astype(jnp.int32)
    table = coeff_table.T
    patch_of, offset_of = patches.transpose(0, 2, 1), offsets.transpose(0, 2, 3, 1)
    own_y, wts_y = blur_half(0, psf_index, table, basis_taps, patch_of, offset_of, image, variance)
    own_x, wts_x = blur_half(1, psf_index, table, basis_taps, patch_of, offset_of, image, variance)

    left_y, right_y = shift(own_y, "y", 1), shift(own_y, "y", -1)
    left_x, right_x = shift(own_x, "x", 1), shift(own_x, "x", -1)
    weights = jnp.concatenate([wts_y[:, 0], wts_x[:, 0]])
    pairs = pairs_of_patch(weights, patches, offsets)
    left_y, right_y, left_x, right_x, pairs = lax.optimization_barrier((left_y, right_y, left_x, right_x, pairs))

    low_y, high_y, low_x, high_x = halves(left_y, right_y, left_x, right_x)
    far = [(0, 0, shift(low_y, "y", 1)), (0, HALF // 2, shift(high_y, "y", -1)),
           (1, 0, shift(low_x, "x", 1)), (1, HALF // 2, shift(high_x, "x", -1))]
    mine, theirs = place(here, [(0, 0, own_y), (0, 0, left_y), (0, 0, right_y),
                                (1, 0, own_x), (1, 0, left_x), (1, 0, right_x)], both=True, cost=12)
    far_arrays, mine, theirs = lax.optimization_barrier(([a for _, _, a in far], mine, theirs))

    received = shift(theirs, "core", 1)
    far = [(group, tile, a) for (group, tile, _), a in zip(far, far_arrays)]
    sib = [(group, tile, shift(a, "core", 1)) for group, tile, a in far]
    denominator = weight_sums(pairs, strip)
    mine, = place(here, far, (mine,))
    ready = place(here, sib, (mine, received), last=True)

    right_a, left_a, low_a, high_a, stay_a, right_b, left_b, low_b, high_b, stay_b = ready
    from_left_a, from_right_a = shift(right_a, "x", 1), shift(left_a, "x", -1)
    from_left_b, from_right_b = shift(right_b, "y", 1), shift(left_b, "y", -1)
    from_left_a, from_right_a, from_left_b, from_right_b = lax.optimization_barrier(
        (from_left_a, from_right_a, from_left_b, from_right_b))
    low_a, low_b, high_a, high_b = add_received(
        (low_a, low_b, high_a, high_b),
        (from_left_a, from_left_b, from_right_a, from_right_b))
    partial = join(stay_a, stay_b,
                   from_left_a, from_right_a, shift(low_a, "x", 1), shift(high_a, "x", -1),
                   from_left_b, from_right_b, shift(low_b, "y", 1), shift(high_b, "y", -1))
    partial = partial.reshape(NZ, 2 * STRIP, PIX)
    total = lax.all_to_all(partial, "z", 0, 0, tiled=True).sum(axis=0)
    numerator = jnp.concatenate([total[:STRIP], total[STRIP:]], axis=1)
    return (numerator / (denominator + 1.0))[None]


def solution(mesh):
    fine = Mesh(mesh.devices.reshape(NX, NZ, NC, NY), ("x", "z", "core", "y"))
    own = ("x", "z", "core")
    return jax.shard_map(
        body,
        mesh=fine,
        in_specs=(
            P("y", own, None, None),
            P("y", own, None, None),
            P("y", own, None),
            P("y", own, None, None),
            P("y", own),
            P(),
            P(),
        ),
        out_specs=P(own, "y", None),
        check_vma=False,
    )
```

```python
import functools

import jax
import jax.numpy as jnp
from jax import lax
from jax.experimental import pallas as pl
from jax.experimental.pallas import tpu as pltpu
from jax.sharding import Mesh
from jax.sharding import PartitionSpec as P

PIX = 128
PATCH_PIX = 256
TAPS = 21
MARGIN = TAPS // 2
NB = 3
NX, NZ, NC, NY = 4, 8, 2, 4
RING = 4
STRIP = PATCH_PIX // NY
TILES = 24
HALF = 12
UNROLL = 3
META = 8
PATCH, ROW, COL, RANK, WEIGHT = range(5)
GROUP_ROWS = META + HALF * PIX
ENTRIES = NZ * NC
ENTRY_ROWS = 2 * STRIP
SLOTS = 32
F32 = jnp.float32
BF16 = jnp.bfloat16
BLUR_LIMIT = 56 * 1024 * 1024
PLACE_LIMIT = 24 * 1024 * 1024
ADD_LIMIT = 12 * 1024 * 1024


def split(value):
    high = value.astype(BF16)
    return high, (value - high.astype(F32)).astype(BF16)


def dot(a, b):
    return jnp.dot(a, b, preferred_element_type=F32)


def blur_kernel(first, psf_ref, table_ref, taps_ref, patch_ref, offset_ref, img_ref, var_ref, out_ref,
                col_hi, col_lo, rows):
    major = lax.broadcasted_iota(jnp.int32, (PIX, PIX), 0)
    minor = lax.broadcasted_iota(jnp.int32, (PIX, PIX), 1)
    for b in range(NB):
        lanes = slice(b * PIX, (b + 1) * PIX)
        for axis, diff in ((0, minor - major), (1, major - minor)):
            band = jnp.zeros((PIX, PIX), F32)
            for t in range(TAPS):
                band = jnp.where(diff == t - MARGIN, taps_ref[b, axis, t], band)
            hi, lo = split(band)
            if axis:
                col_hi[:PIX, lanes], col_hi[PIX:, lanes], col_lo[:, lanes] = hi, hi, lo
            else:
                rows[:PIX, lanes], rows[PIX:, lanes] = hi, lo

    x_hi, x_lo = split(img_ref[0].reshape(HALF * PIX, PIX))
    smooth = dot(jnp.concatenate([x_hi, x_lo], axis=1), col_hi[...]) + dot(x_hi, col_lo[...])
    weights = []
    for n in range(HALF):
        total = jnp.sum(jnp.sum(var_ref[0, n], axis=0, keepdims=True), axis=1, keepdims=True)
        weights.append(1.0 / (total * (1.0 / (PIX * PIX))))
    for pair in range(HALF // 2):
        sides = []
        for n in (2 * pair, 2 * pair + 1):
            row = psf_ref[0, first + n]
            sides.append(jnp.concatenate(
                [smooth[n * PIX:(n + 1) * PIX, b * PIX:(b + 1) * PIX] * (table_ref[b, row] * weights[n])
                 for b in range(NB)], axis=0))
        q_hi, q_lo = split(jnp.concatenate(sides, axis=1))
        both = dot(rows[...], q_hi)
        done = both[:PIX] + (both[PIX:] + dot(rows[:PIX], q_lo))
        for n in range(2):
            at = META + (2 * pair + n) * PIX
            out_ref[at:at + PIX, :] = done[:, n * PIX:(n + 1) * PIX]

    lane = lax.broadcasted_iota(jnp.int32, (META, PIX), 1)
    kind = lax.broadcasted_iota(jnp.int32, (META, PIX), 0)
    patch, facts = jnp.zeros((META, PIX), jnp.int32), jnp.zeros((META, PIX), jnp.int32)
    for t in range(TILES):
        for k in range(2):
            here = lane == 2 * t + k
            patch = jnp.where(here, patch_ref[0, k, t], patch)
            place = jnp.where(kind == ROW, offset_ref[0, k, 0, t], offset_ref[0, k, 1, t])
            facts = jnp.where(here, place, facts)
    rank = jnp.zeros((META, PIX), jnp.int32)
    for t in range(TILES):
        for k in range(2):
            rank += jnp.where((patch == patch_ref[0, k, t]) & (lane > 2 * t + k), 1, 0)
    facts = jnp.where(kind == PATCH, patch, jnp.where(kind == RANK, rank, facts)).astype(F32)
    for n in range(HALF):
        facts = jnp.where((kind == WEIGHT) & ((lane >> 1) == first + n), weights[n], facts)
    out_ref[0:META, :] = facts


def blur_half(half, psf_index, table, taps, patches, offsets, image, variance):
    smem = pl.BlockSpec(memory_space=pltpu.SMEM)
    tiles = pl.BlockSpec((1, HALF, PIX, PIX), lambda i: (0, half, 0, 0))
    return pl.pallas_call(
        functools.partial(blur_kernel, half * HALF),
        grid=(1,),
        in_specs=[smem] * 5 + [tiles, tiles],
        out_specs=pl.BlockSpec((GROUP_ROWS, PIX), lambda i: (0, 0)),
        out_shape=pltpu.VMEM((GROUP_ROWS, PIX), F32),
        scratch_shapes=[pltpu.VMEM((2 * PIX, NB * PIX), BF16), pltpu.VMEM((PIX, NB * PIX), BF16),
                        pltpu.VMEM((2 * PIX, NB * PIX), BF16)],
        compiler_params=pltpu.CompilerParams(vmem_limit_bytes=BLUR_LIMIT),
        cost_estimate=pl.CostEstimate(flops=HALF * 76 * 10**6, bytes_accessed=HALF * 3 * 65536,
                                      transcendentals=0),
        name="blur_half",
    )(psf_index, table, taps, patches, offsets, image, variance)


def place_kernel(runs, last, here_ref, *refs):
    count = len(runs)
    tiles, refs = refs[:count], refs[count:]
    if last:
        old_canvas, old_notes, *outs, canvas, notes = refs[:-5]
    else:
        canvas, notes = refs[:-5]
    buf, whole_facts, whole_ref, weight_ref, sems = refs[-5:]
    copies, starts, at = [], [], STRIP
    for n, source in enumerate(tiles):
        copies.append(pltpu.make_async_copy(source, buf.at[pl.ds(at, GROUP_ROWS)], sems.at[n]))
        copies[n].start()
        buf[at - STRIP:at] = jnp.zeros((STRIP, PIX), F32)
        starts.append(at + META)
        at += GROUP_ROWS + STRIP
    buf[at - STRIP:at] = jnp.zeros((STRIP, PIX), F32)
    if last:
        canvas[...] = old_canvas[...]
        notes[...] = old_notes[...]
    else:
        canvas[...] = jnp.zeros(canvas.shape, F32)
        notes[...] = jnp.zeros(notes.shape, F32)
    my_x, core, my_y = here_ref[0], here_ref[1], here_ref[2]
    to_scalars = []
    for n, copy in enumerate(copies):
        copy.wait()
        rows = pl.ds(n * META, META)
        head = pl.ds(starts[n] - META, META)
        whole_facts[n * META:(n + 1) * META] = buf[starts[n] - META:starts[n]].astype(jnp.int32)
        to_scalars.append(pltpu.make_async_copy(whole_facts.at[rows], whole_ref.at[rows], sems.at[count + n]))
        to_scalars.append(pltpu.make_async_copy(buf.at[head], weight_ref.at[rows], sems.at[2 * count + n]))
        for scalars in to_scalars[-2:]:
            scalars.start()
    for scalars in to_scalars:
        scalars.wait()
    row_of = lax.broadcasted_iota(jnp.int32, (8, PIX), 0)
    lane = lax.broadcasted_iota(jnp.int32, (8, PIX), 1)
    lane_one = lax.broadcasted_iota(jnp.int32, (1, PIX), 1)

    def add(items):
        moved = [pltpu.roll(buf[pl.ds(tile_row + skip, STRIP), :], (col + PIX) & (PIX - 1), 1)
                 for _, tile_row, skip, col in items]
        for (at, _, skip, col), strip in zip(items, moved):
            sides = [(lane >= col - n * PIX) & (lane < col - n * PIX + PIX) for n in range(2)]
            for g in range(0, STRIP, 8):
                line = row_of + (skip + g)
                inside = (line >= 0) & (line < PIX)
                for n in range(2):
                    canvas[at, n, g:g + 8] += jnp.where(inside & sides[n], strip[g:g + 8], 0.0)

    def bounded(skip):
        return jnp.clip(skip, -STRIP, PIX)

    def pair_of(index, pair, reduce_at, source_at):
        patch, row, col, rank = (whole_ref[index * META + kind, pair] for kind in (PATCH, ROW, COL, RANK))
        weight = weight_ref[index * META + WEIGHT, pair]
        slot = reduce_at * (2 * RING) + source_at * 2 + rank
        note = jnp.where(lane_one == slot, weight, 0.0)
        note = jnp.where(lane_one == slot + SLOTS, row, note.astype(jnp.int32) * 0).astype(F32) + note
        note = jnp.where(lane_one == slot + 2 * SLOTS, col, 0).astype(F32) + note
        return patch, row, col, note

    def along_y(t, carry, index, pair, base, steps):
        items = []
        for n in range(UNROLL):
            for k in range(2):
                patch, row, col, note = pair_of(index, pair + 2 * (UNROLL * t + n) + k, my_x,
                                                (my_y + steps) & (RING - 1))
                at = (((patch >> 4) - my_x) & (RING - 1)) * ENTRIES + (patch & (ENTRIES - 1))
                notes[pl.ds(at, 1), :] += note
                items.append((at, base + (UNROLL * t + n) * PIX, bounded(my_y * STRIP - row), col))
        add(items)
        return carry

    def along_x(t, carry, index, pair, base, steps):
        for k in range(2):
            @pl.when((whole_ref[index * META + PATCH, pair + 2 * t + k] >> 4) == my_x)
            def _():
                patch, row, col, note = pair_of(index, pair + 2 * t + k, my_y, (my_x + steps) & (RING - 1))
                for n in range(NY):
                    notes[pl.ds(n * ENTRIES + (patch & (ENTRIES - 1)), 1), :] += note
                items = []
                for n in range(3):
                    strip = (jnp.maximum(row, 0) >> 6) + n
                    skip = jnp.where(strip < NY, bounded(strip * STRIP - row), PIX)
                    at = ((strip - my_y) & (RING - 1)) * ENTRIES + (patch & (ENTRIES - 1))
                    items.append((at, base + t * PIX, skip, col))
                add(items)
        return carry

    def each_run(step, number):
        for index, (half, steps) in enumerate(runs):
            given = dict(index=index, pair=2 * HALF * half, base=starts[index], steps=steps)
            lax.fori_loop(0, number, functools.partial(step, **given), 0)

    @pl.when(core == 0)
    def _():
        each_run(along_y, HALF // UNROLL)

    @pl.when(core == 1)
    def _():
        each_run(along_x, HALF)

    if last:
        for n, out in enumerate(outs):
            size = ENTRIES // 2
            out[:size * ENTRY_ROWS] = canvas[n * size:(n + 1) * size].reshape(size * ENTRY_ROWS, PIX)
            out[size * ENTRY_ROWS:] = notes[n * size:(n + 1) * size]


def place(here, arrays, runs, old=(), cost=6):
    smem = pl.BlockSpec(memory_space=pltpu.SMEM)
    hbm = pl.BlockSpec(memory_space=pl.ANY)
    vmem = pl.BlockSpec(memory_space=pltpu.VMEM)
    canvas, notes = (RING * ENTRIES, 2, STRIP, PIX), (RING * ENTRIES, PIX)
    part = (ENTRIES // 2 * ENTRY_ROWS + ENTRIES // 2, PIX)
    count = len(arrays)
    outs = [part] * (2 * RING) if old else [canvas, notes]
    return pl.pallas_call(
        functools.partial(place_kernel, tuple(runs), bool(old)),
        in_specs=[smem] + [hbm] * count + [vmem] * len(old),
        out_specs=[vmem] * len(outs),
        out_shape=[pltpu.VMEM(shape, F32) for shape in outs],
        scratch_shapes=([pltpu.VMEM(canvas, F32), pltpu.VMEM(notes, F32)] if old else [])
        + [pltpu.VMEM((count * (GROUP_ROWS + STRIP) + STRIP, PIX), F32),
           pltpu.VMEM((count * META, PIX), jnp.int32),
           pltpu.SMEM((count * META, PIX), jnp.int32),
           pltpu.SMEM((count * META, PIX), F32),
           pltpu.SemaphoreType.DMA((3 * count,))],
        compiler_params=pltpu.CompilerParams(vmem_limit_bytes=PLACE_LIMIT),
        cost_estimate=pl.CostEstimate(flops=10**6, bytes_accessed=cost * 3690000, transcendentals=0),
        name="place",
    )(here, *arrays, *old)


def add_kernel(a, b, c, d, first, second):
    first[...] = a[...] + b[...]
    second[...] = c[...] + d[...]


def add_received(*arrays):
    vmem = pl.BlockSpec(memory_space=pltpu.VMEM)
    return pl.pallas_call(
        add_kernel,
        in_specs=[vmem] * 4,
        out_specs=[vmem] * 2,
        out_shape=[pltpu.VMEM(arrays[0].shape, F32)] * 2,
        compiler_params=pltpu.CompilerParams(vmem_limit_bytes=ADD_LIMIT),
        name="add_received",
    )(*arrays)


def join_kernel(here_ref, low_a, low_b, low_c, high_a, high_b, high_c, mine, theirs, total):
    core = here_ref[1]
    size = ENTRIES // 2
    for n, (a, b, c) in enumerate(((low_a, low_b, low_c), (high_a, high_b, high_c))):
        start = n * size * (ENTRY_ROWS + 1)
        total[start:start + size * (ENTRY_ROWS + 1)] = a[...] + b[...] + c[...]
    kind = lax.broadcasted_iota(jnp.int32, (8, PIX), 0)
    for out, parity in ((mine, core), (theirs, 1 - core)):
        for column in range(NZ):
            half, entry = column // (NZ // 2), NC * (column % (NZ // 2)) + parity
            start = half * size * (ENTRY_ROWS + 1)
            out[column, :ENTRY_ROWS] = total[pl.ds(pl.multiple_of(start + entry * ENTRY_ROWS, 8), ENTRY_ROWS), :]
            note = total[pl.ds(start + size * ENTRY_ROWS + entry, 1), :]
            out[column, ENTRY_ROWS:] = jnp.where(kind == core, note, 0.0)


def join(here, *arrays):
    vmem = pl.BlockSpec(memory_space=pltpu.VMEM)
    return pl.pallas_call(
        join_kernel,
        in_specs=[pl.BlockSpec(memory_space=pltpu.SMEM)] + [vmem] * 6,
        out_specs=[vmem] * 2,
        out_shape=[pltpu.VMEM((NZ, ENTRY_ROWS + 8, PIX), F32)] * 2,
        scratch_shapes=[pltpu.VMEM((ENTRIES * (ENTRY_ROWS + 1), PIX), F32)],
        compiler_params=pltpu.CompilerParams(vmem_limit_bytes=ADD_LIMIT),
        name="join",
    )(here, *arrays)


def finish_kernel(here_ref, got, out):
    my_y = here_ref[2]
    lane = lax.broadcasted_iota(jnp.int32, (1, PIX), 1)
    row_of = lax.broadcasted_iota(jnp.int32, (STRIP, PIX), 0)
    col_of = lax.broadcasted_iota(jnp.int32, (PATCH_PIX, PIX), 0)
    highs, mids, lows, hits = [], [], [], []
    for column in range(NZ):
        for core in range(NC):
            note = got[column, ENTRY_ROWS + core:ENTRY_ROWS + core + 1, :]
            weight = jnp.where(lane < SLOTS, note, 0.0)
            row = pltpu.roll(note, PIX - SLOTS, 1).astype(jnp.int32) - my_y * STRIP
            col = pltpu.roll(note, PIX - 2 * SLOTS, 1).astype(jnp.int32)
            line, pixel = row_of - row, col_of - col
            hit = (line >= 0) & (line < PIX)
            high, rest = split(weight)
            mid, low = split(weight - high.astype(F32))
            for many, piece in ((highs, high), (mids, mid), (lows, low)):
                many.append(jnp.where(hit, jnp.broadcast_to(piece.astype(F32), hit.shape), 0.0).astype(BF16))
            hits.append(jnp.where((pixel >= 0) & (pixel < PIX), 1.0, 0.0).astype(BF16))
    left = jnp.concatenate([jnp.concatenate(many, axis=1) for many in (highs, mids, lows)], axis=0)
    sums = lax.dot_general(left, jnp.concatenate(hits, axis=1), (((1,), (1,)), ((), ())),
                           preferred_element_type=F32)
    denominator = sums[:STRIP] + (sums[STRIP:2 * STRIP] + sums[2 * STRIP:]) + 1.0
    for side in range(2):
        rows = slice(side * STRIP, (side + 1) * STRIP)
        total = got[0, rows]
        for column in range(1, NZ):
            total = total + got[column, rows]
        lanes = slice(side * PIX, (side + 1) * PIX)
        out[:, lanes] = total / denominator[:, lanes]


def finish(here, got):
    vmem = pl.BlockSpec(memory_space=pltpu.VMEM)
    return pl.pallas_call(
        finish_kernel,
        in_specs=[pl.BlockSpec(memory_space=pltpu.SMEM), vmem],
        out_specs=vmem,
        out_shape=jax.ShapeDtypeStruct((STRIP, PATCH_PIX), F32),
        compiler_params=pltpu.CompilerParams(vmem_limit_bytes=ADD_LIMIT),
        name="finish",
    )(here, got)


def shift(value, along, by):
    pairs = []
    for x in range(NX):
        for core in range(NC):
            for y in range(NY):
                to = dict(x=x, y=y)
                to[along[core]] = (to[along[core]] + by) % RING
                pairs.append(((x * NC + core) * NY + y, (to["x"] * NC + core) * NY + to["y"]))
    return lax.ppermute(value, ("x", "core", "y"), pairs)


def body(image, variance, patches, offsets, psf_index, coeff_table, basis_taps):
    here = jnp.stack([lax.axis_index(axis) for axis in ("x", "core", "y")]).astype(jnp.int32)
    given = (psf_index, coeff_table.T, basis_taps, patches.transpose(0, 2, 1), offsets.transpose(0, 2, 3, 1),
             image, variance)

    own = [blur_half(half, *given) for half in range(2)]
    left = [shift(a, "yx", 1) for a in own]
    right = [shift(a, "yx", -1) for a in own]
    far = [shift(left[0], "yx", 1), shift(right[1], "yx", -1)]
    held = place(here, (*own, *left, *right), [(half, steps) for steps in (0, -1, 1) for half in range(2)], cost=9)
    far, held = lax.optimization_barrier((far, held))
    parts = place(here, far, [(0, 2), (1, 2)], held)

    stay_low, stay_high, right_low, right_high, far_low, far_high, left_low, left_high = parts
    from_left, from_right = shift(far_low, "xy", 1), shift(far_high, "xy", -1)
    high, low = shift(right_high, "xy", 1), shift(left_low, "xy", -1)
    right_low, left_high = add_received(right_low, from_left, left_high, from_right)
    mine, theirs = join(here, stay_low, low, shift(right_low, "xy", 1), stay_high, high, shift(left_high, "xy", -1))
    mine = mine + lax.ppermute(theirs, "core", [(0, 1), (1, 0)])
    got = lax.all_to_all(mine, "z", 0, 0, tiled=True)
    return finish(here, got)[None]


def solution(mesh):
    fine = Mesh(mesh.devices.reshape(NX, NZ, NC, NY), ("x", "z", "core", "y"))
    own = ("x", "z", "core")
    return jax.shard_map(
        body,
        mesh=fine,
        in_specs=(
            P("y", own, None, None),
            P("y", own, None, None),
            P("y", own, None),
            P("y", own, None, None),
            P("y", own),
            P(),
            P(),
        ),
        out_specs=P(own, "y", None),
        check_vma=False,
    )
```

```python
import functools

import jax
import jax.numpy as jnp
from jax import lax
from jax.experimental import pallas as pl
from jax.experimental.pallas import tpu as pltpu
from jax.sharding import Mesh
from jax.sharding import PartitionSpec as P

PIX = 128
PATCH_PIX = 256
TAPS = 21
MARGIN = TAPS // 2
NB = 3
NX, NZ, NC, NY = 4, 8, 2, 4
RING = 4
STRIP = PATCH_PIX // NY
TILES = 24
PARTS = ((0, 12), (12, 12))
UNROLL = 3
META = 8
PATCH, ROW, COL, RANK, WEIGHT = range(5)
ENTRIES = NZ * NC
ENTRY_ROWS = 2 * STRIP
SLOTS = 32
STEPS = (1, 2, 3, -1, -2, -3)
LAST = ((0, 8), (4, 12), (32, 36), (40, 44), (24,), (28,), (48,), (52,), (16, 20), (56, 60))
F32 = jnp.float32
BF16 = jnp.bfloat16
BLUR_LIMIT = 56 * 1024 * 1024
PLACE_LIMIT = 24 * 1024 * 1024
ADD_LIMIT = 12 * 1024 * 1024


def split(value):
    high = value.astype(BF16)
    return high, (value - high.astype(F32)).astype(BF16)


def dot(a, b):
    return jnp.dot(a, b, preferred_element_type=F32)


def blur_kernel(first, tiles, psf_ref, table_ref, taps_ref, patch_ref, offset_ref, img_ref, var_ref, out_ref,
                col_hi, col_lo, rows):
    major = lax.broadcasted_iota(jnp.int32, (PIX, PIX), 0)
    minor = lax.broadcasted_iota(jnp.int32, (PIX, PIX), 1)
    for b in range(NB):
        lanes = slice(b * PIX, (b + 1) * PIX)
        for axis, diff in ((0, minor - major), (1, major - minor)):
            band = jnp.zeros((PIX, PIX), F32)
            for t in range(TAPS):
                band = jnp.where(diff == t - MARGIN, taps_ref[b, axis, t], band)
            hi, lo = split(band)
            if axis:
                col_hi[:PIX, lanes], col_hi[PIX:, lanes], col_lo[:, lanes] = hi, hi, lo
            else:
                rows[:PIX, lanes], rows[PIX:, lanes] = hi, lo

    x_hi, x_lo = split(img_ref[0].reshape(tiles * PIX, PIX))
    smooth = dot(jnp.concatenate([x_hi, x_lo], axis=1), col_hi[...]) + dot(x_hi, col_lo[...])
    weights = []
    for n in range(tiles):
        total = jnp.sum(jnp.sum(var_ref[0, n], axis=0, keepdims=True), axis=1, keepdims=True)
        weights.append(1.0 / (total * (1.0 / (PIX * PIX))))
    for pair in range(tiles // 2):
        sides = []
        for n in (2 * pair, 2 * pair + 1):
            row = psf_ref[0, first + n]
            sides.append(jnp.concatenate(
                [smooth[n * PIX:(n + 1) * PIX, b * PIX:(b + 1) * PIX] * (table_ref[b, row] * weights[n])
                 for b in range(NB)], axis=0))
        q_hi, q_lo = split(jnp.concatenate(sides, axis=1))
        both = dot(rows[...], q_hi)
        done = both[:PIX] + (both[PIX:] + dot(rows[:PIX], q_lo))
        for n in range(2):
            at = META + (2 * pair + n) * PIX
            out_ref[at:at + PIX, :] = done[:, n * PIX:(n + 1) * PIX]

    lane = lax.broadcasted_iota(jnp.int32, (META, PIX), 1)
    kind = lax.broadcasted_iota(jnp.int32, (META, PIX), 0)
    patch, facts = jnp.zeros((META, PIX), jnp.int32), jnp.zeros((META, PIX), jnp.int32)
    for t in range(TILES):
        for k in range(2):
            here = lane == 2 * t + k
            patch = jnp.where(here, patch_ref[0, k, t], patch)
            place = jnp.where(kind == ROW, offset_ref[0, k, 0, t], offset_ref[0, k, 1, t])
            facts = jnp.where(here, place, facts)
    rank = jnp.zeros((META, PIX), jnp.int32)
    for t in range(TILES):
        for k in range(2):
            rank += jnp.where((patch == patch_ref[0, k, t]) & (lane > 2 * t + k), 1, 0)
    facts = jnp.where(kind == PATCH, patch, jnp.where(kind == RANK, rank, facts)).astype(F32)
    for n in range(tiles):
        facts = jnp.where((kind == WEIGHT) & ((lane >> 1) == first + n), weights[n], facts)
    out_ref[0:META, :] = facts


def blur_part(part, psf_index, table, taps, patches, offsets, image, variance):
    first, tiles = PARTS[part]
    smem = pl.BlockSpec(memory_space=pltpu.SMEM)
    block = pl.BlockSpec((1, tiles, PIX, PIX), lambda i: (0, first // tiles, 0, 0))
    rows = META + tiles * PIX
    return pl.pallas_call(
        functools.partial(blur_kernel, first, tiles),
        grid=(1,),
        in_specs=[smem] * 5 + [block, block],
        out_specs=pl.BlockSpec((rows, PIX), lambda i: (0, 0)),
        out_shape=pltpu.VMEM((rows, PIX), F32),
        scratch_shapes=[pltpu.VMEM((2 * PIX, NB * PIX), BF16), pltpu.VMEM((PIX, NB * PIX), BF16),
                        pltpu.VMEM((2 * PIX, NB * PIX), BF16)],
        compiler_params=pltpu.CompilerParams(vmem_limit_bytes=BLUR_LIMIT),
        cost_estimate=pl.CostEstimate(flops=tiles * 76 * 10**6, bytes_accessed=tiles * 3 * 65536,
                                      transcendentals=0),
        name="blur_part",
    )(psf_index, table, taps, patches, offsets, image, variance)


def place_kernel(runs, held, last, here_ref, *refs):
    count = len(runs)
    tiles, refs = refs[:count], refs[count:]
    if held:
        old_canvas, old_notes, *refs = refs
    *outs, canvas, notes = refs[:-6]
    buf, whole_facts, whole_ref, weight_ref, list_ref, sems = refs[-6:]
    copies, starts, at = [], [], STRIP
    for n, source in enumerate(tiles):
        copies.append(pltpu.make_async_copy(source, buf.at[pl.ds(at, source.shape[0])], sems.at[n]))
        copies[n].start()
        buf[at - STRIP:at] = jnp.zeros((STRIP, PIX), F32)
        starts.append(at + META)
        at += source.shape[0] + STRIP
    buf[at - STRIP:at] = jnp.zeros((STRIP, PIX), F32)
    if held:
        canvas[...] = old_canvas[...]
        notes[...] = old_notes[...]
    else:
        canvas[...] = jnp.zeros(canvas.shape, F32)
        notes[...] = jnp.zeros(notes.shape, F32)
    my_x, core, my_y = here_ref[0], here_ref[1], here_ref[2]
    to_scalars = []
    for n, copy in enumerate(copies):
        copy.wait()
        rows = pl.ds(n * META, META)
        head = pl.ds(starts[n] - META, META)
        whole_facts[n * META:(n + 1) * META] = buf[starts[n] - META:starts[n]].astype(jnp.int32)
        to_scalars.append(pltpu.make_async_copy(whole_facts.at[rows], whole_ref.at[rows], sems.at[count + n]))
        to_scalars.append(pltpu.make_async_copy(buf.at[head], weight_ref.at[rows], sems.at[2 * count + n]))
        for scalars in to_scalars[-2:]:
            scalars.start()
    for scalars in to_scalars:
        scalars.wait()
    row_of = lax.broadcasted_iota(jnp.int32, (8, PIX), 0)
    lane = lax.broadcasted_iota(jnp.int32, (8, PIX), 1)
    lane_one = lax.broadcasted_iota(jnp.int32, (1, PIX), 1)

    def add(items):
        moved = [pltpu.roll(buf[pl.ds(tile_row + skip, STRIP), :], (col + PIX) & (PIX - 1), 1)
                 for _, tile_row, skip, col in items]
        for (at, _, skip, col), strip in zip(items, moved):
            sides = [(lane >= col - n * PIX) & (lane < col - n * PIX + PIX) for n in range(2)]
            for g in range(0, STRIP, 8):
                line = row_of + (skip + g)
                inside = (line >= 0) & (line < PIX)
                for n in range(2):
                    canvas[at, n, g:g + 8] += jnp.where(inside & sides[n], strip[g:g + 8], 0.0)

    def bounded(skip):
        return jnp.clip(skip, -STRIP, PIX)

    def pair_of(index, pair, slot):
        patch, row, col, rank = (whole_ref[index * META + kind, pair] for kind in (PATCH, ROW, COL, RANK))
        weight = weight_ref[index * META + WEIGHT, pair]
        slot = slot + rank
        place = jnp.where(lane_one == slot + SLOTS, row, jnp.where(lane_one == slot + 2 * SLOTS, col, 0))
        return patch, row, col, jnp.where(lane_one == slot, weight, place.astype(F32))

    def entry_of(patch):
        z = (patch >> 1) & (NZ - 1)
        return (z >> 2) * NZ + ((patch & 1) ^ core) * (NZ // 2) + (z & (NZ // 2 - 1))

    def slot_of(reduce_at, source_at):
        return reduce_at * (2 * RING) + (source_at & (RING - 1)) * 2

    def along_y(t, carry, index, pair, base, steps):
        items = []
        for n in range(UNROLL):
            for k in range(2):
                patch, row, col, note = pair_of(index, pair + 2 * (UNROLL * t + n) + k, slot_of(my_x, my_y + steps))
                at = (((patch >> 4) - my_x) & (RING - 1)) * ENTRIES + entry_of(patch)
                notes[pl.ds(at, 1), :] += note
                items.append((at, base + (UNROLL * t + n) * PIX, bounded(my_y * STRIP - row), col))
        add(items)
        return carry

    def list_x(t, number, index, pair, base, steps):
        for n in range(UNROLL):
            for k in range(2):
                lane_of = pair + 2 * (UNROLL * t + n) + k
                list_ref[0, number] = index * PIX + lane_of
                list_ref[1, number] = base + (UNROLL * t + n) * PIX
                list_ref[2, number] = slot_of(my_y, my_x + steps)
                number += jnp.where((whole_ref[index * META + PATCH, lane_of] >> 4) == my_x, 1, 0)
        return number

    def along_x(t, number):
        items = []
        for k in range(2):
            valid = 2 * t + k < number
            at = jnp.minimum(2 * t + k, number - 1)
            code, tile_row, slot = list_ref[0, at], list_ref[1, at], list_ref[2, at]
            patch, row, col, note = pair_of(code >> 7, code & (PIX - 1), jnp.where(valid, slot, PIX))
            for n in range(NY):
                notes[pl.ds(n * ENTRIES + entry_of(patch), 1), :] += note
            for n in range(3):
                strip = (jnp.maximum(row, 0) >> 6) + n
                skip = jnp.where(valid & (strip < NY), bounded(strip * STRIP - row), PIX)
                at = ((strip - my_y) & (RING - 1)) * ENTRIES + entry_of(patch)
                items.append((at, tile_row, skip, col))
        add(items)
        return number

    given = [(PARTS[part][1] // UNROLL, dict(index=n, pair=2 * PARTS[part][0], base=starts[n], steps=steps))
             for n, (part, steps) in enumerate(runs)]

    @pl.when(core == 0)
    def _():
        for groups, run in given:
            lax.fori_loop(0, groups, functools.partial(along_y, **run), 0)

    @pl.when(core == 1)
    def _():
        number = 0
        for groups, run in given:
            number = lax.fori_loop(0, groups, functools.partial(list_x, **run), number)
        lax.fori_loop(0, (number + 1) >> 1, along_x, number)

    if last:
        for out, first in zip(outs, LAST):
            at = 0
            for start in first:
                out[at * ENTRY_ROWS:(at + 4) * ENTRY_ROWS] = canvas[start:start + 4].reshape(4 * ENTRY_ROWS, PIX)
                out[len(first) * 4 * ENTRY_ROWS + at:len(first) * 4 * ENTRY_ROWS + at + 4] = notes[start:start + 4]
                at += 4


def place(here, arrays, runs, old=(), last=False, cost=6):
    smem = pl.BlockSpec(memory_space=pltpu.SMEM)
    hbm = pl.BlockSpec(memory_space=pl.ANY)
    vmem = pl.BlockSpec(memory_space=pltpu.VMEM)
    canvas, notes = (RING * ENTRIES, 2, STRIP, PIX), (RING * ENTRIES, PIX)
    count, rows = len(arrays), sum(a.shape[0] + STRIP for a in arrays) + STRIP
    outs = [canvas, notes]
    if last:
        outs = [(len(first) * 4 * ENTRY_ROWS + 8, PIX) for first in LAST]
    return pl.pallas_call(
        functools.partial(place_kernel, tuple(runs), bool(old), last),
        in_specs=[smem] + [hbm] * count + [vmem] * len(old),
        out_specs=[vmem] * len(outs),
        out_shape=[pltpu.VMEM(shape, F32) for shape in outs],
        scratch_shapes=([pltpu.VMEM(canvas, F32), pltpu.VMEM(notes, F32)] if last else [])
        + [pltpu.VMEM((rows, PIX), F32),
           pltpu.VMEM((count * META, PIX), jnp.int32),
           pltpu.SMEM((count * META, PIX), jnp.int32),
           pltpu.SMEM((count * META, PIX), F32),
           pltpu.SMEM((3, count * 2 * TILES), jnp.int32),
           pltpu.SemaphoreType.DMA((3 * count,))],
        compiler_params=pltpu.CompilerParams(vmem_limit_bytes=PLACE_LIMIT),
        cost_estimate=pl.CostEstimate(flops=10**6, bytes_accessed=cost * 3690000, transcendentals=0),
        name="place",
    )(here, *arrays, *old)


def add_kernel(a, b, c, d, *outs):
    size = 4 * ENTRY_ROWS
    for n, (one, other) in enumerate(((a, b), (c, d))):
        for k in range(2):
            out = outs[2 * n + k]
            out[:size] = one[k * size:(k + 1) * size] + other[k * size:(k + 1) * size]
            rows = slice(2 * size + 4 * k, 2 * size + 4 * k + 4)
            out[size:size + 4] = one[rows] + other[rows]


def add_received(*arrays):
    vmem = pl.BlockSpec(memory_space=pltpu.VMEM)
    return pl.pallas_call(
        add_kernel,
        in_specs=[vmem] * 4,
        out_specs=[vmem] * 4,
        out_shape=[pltpu.VMEM((4 * ENTRY_ROWS + 8, PIX), F32)] * 4,
        compiler_params=pltpu.CompilerParams(vmem_limit_bytes=ADD_LIMIT),
        name="add_received",
    )(*arrays)


def join_kernel(here_ref, stay, stay_cross, *refs):
    arrays, outs, total, note_sums = refs[:8], refs[8:17], refs[17], refs[18]
    core, my_z = here_ref[1], here_ref[3]
    size = 4 * ENTRY_ROWS
    for half in range(2):
        rows = slice(half * size, (half + 1) * size)
        same, cross = arrays[2 * half:2 * half + 2], arrays[4 + 2 * half:6 + 2 * half]
        total[rows] = ((stay[rows] + stay_cross[rows]) + (same[0][:size] + same[1][:size])
                       + (cross[0][:size] + cross[1][:size]))
        head = slice(2 * size + 4 * half, 2 * size + 4 * half + 4)
        for n, (first, rest) in enumerate(((stay, same), (stay_cross, cross))):
            note_sums[8 * n + 4 * half:8 * n + 4 * half + 4] = (
                first[head] + (rest[0][size:size + 4] + rest[1][size:size + 4]))
    kind = lax.broadcasted_iota(jnp.int32, (8, PIX), 0)

    def rows_of(steps, start, count):
        owner = (my_z + steps) & (NZ - 1)
        return total[pl.ds(pl.multiple_of(owner * ENTRY_ROWS + start, 8), count), :]

    def notes_of(steps, row):
        owner = (my_z + steps) & (NZ - 1)
        same, cross = (note_sums[pl.ds(8 * n + owner, 1), :] for n in range(2))
        return jnp.where(kind == row + core, same, jnp.where(kind == row + 1 - core, cross, 0.0))

    for out, steps in zip(outs, (0, *STEPS)):
        out[:ENTRY_ROWS] = rows_of(steps, 0, ENTRY_ROWS)
        out[ENTRY_ROWS:] = notes_of(steps, 0)
    outs[7][...] = rows_of(4, 0, STRIP)
    outs[8][:STRIP] = rows_of(4, STRIP, STRIP)
    outs[8][STRIP:] = notes_of(4, NC)


def join(here, *arrays):
    vmem = pl.BlockSpec(memory_space=pltpu.VMEM)
    rows = [ENTRY_ROWS + 8] * 7 + [STRIP, STRIP + 8]
    return pl.pallas_call(
        join_kernel,
        in_specs=[pl.BlockSpec(memory_space=pltpu.SMEM)] + [vmem] * 10,
        out_specs=[vmem] * 9,
        out_shape=[pltpu.VMEM((n, PIX), F32) for n in rows],
        scratch_shapes=[pltpu.VMEM((NZ * ENTRY_ROWS, PIX), F32), pltpu.VMEM((2 * NZ, PIX), F32)],
        compiler_params=pltpu.CompilerParams(vmem_limit_bytes=ADD_LIMIT),
        name="join",
    )(here, *arrays)


def relay_kernel(ahead, behind, from_left, from_right, ahead_out, behind_out):
    ahead_out[:STRIP] = ahead[:STRIP] + from_left[...]
    ahead_out[STRIP:] = ahead[STRIP:]
    behind_out[:STRIP] = behind[:STRIP]
    behind_out[STRIP:] = behind[STRIP:] + from_right[...]


def relay(*arrays):
    vmem = pl.BlockSpec(memory_space=pltpu.VMEM)
    return pl.pallas_call(
        relay_kernel,
        in_specs=[vmem] * 4,
        out_specs=[vmem] * 2,
        out_shape=[pltpu.VMEM(arrays[0].shape, F32)] * 2,
        compiler_params=pltpu.CompilerParams(vmem_limit_bytes=ADD_LIMIT),
        name="relay",
    )(*arrays)


def finish_kernel(here_ref, *refs):
    *got, out = refs
    my_y = here_ref[2]
    lane = lax.broadcasted_iota(jnp.int32, (1, PIX), 1)
    row_of = lax.broadcasted_iota(jnp.int32, (STRIP, PIX), 0)
    col_of = lax.broadcasted_iota(jnp.int32, (PATCH_PIX, PIX), 0)
    highs, mids, lows, hits = [], [], [], []
    for source in (*got, got[-1]):
        for core in range(NC):
            at = ENTRY_ROWS + core + (NC if len(hits) >= len(got) * NC else 0)
            note = source[at:at + 1, :]
            weight = jnp.where(lane < SLOTS, note, 0.0)
            row = pltpu.roll(note, PIX - SLOTS, 1).astype(jnp.int32) - my_y * STRIP
            col = pltpu.roll(note, PIX - 2 * SLOTS, 1).astype(jnp.int32)
            line, pixel = row_of - row, col_of - col
            hit = (line >= 0) & (line < PIX)
            high, rest = split(weight)
            mid, low = split(weight - high.astype(F32))
            for many, piece in ((highs, high), (mids, mid), (lows, low)):
                many.append(jnp.where(hit, jnp.broadcast_to(piece.astype(F32), hit.shape), 0.0).astype(BF16))
            hits.append(jnp.where((pixel >= 0) & (pixel < PIX), 1.0, 0.0).astype(BF16))
    left = jnp.concatenate([jnp.concatenate(many, axis=1) for many in (highs, mids, lows)], axis=0)
    sums = lax.dot_general(left, jnp.concatenate(hits, axis=1), (((1,), (1,)), ((), ())),
                           preferred_element_type=F32)
    denominator = sums[:STRIP] + (sums[STRIP:2 * STRIP] + sums[2 * STRIP:]) + 1.0
    for side in range(2):
        rows = slice(side * STRIP, (side + 1) * STRIP)
        total = got[0][rows]
        for source in got[1:]:
            total = total + source[rows]
        lanes = slice(side * PIX, (side + 1) * PIX)
        out[:, lanes] = total / denominator[:, lanes]


def finish(here, got):
    vmem = pl.BlockSpec(memory_space=pltpu.VMEM)
    return pl.pallas_call(
        finish_kernel,
        in_specs=[pl.BlockSpec(memory_space=pltpu.SMEM)] + [vmem] * len(got),
        out_specs=vmem,
        out_shape=jax.ShapeDtypeStruct((STRIP, PATCH_PIX), F32),
        compiler_params=pltpu.CompilerParams(vmem_limit_bytes=ADD_LIMIT),
        name="finish",
    )(here, *got)


def shift_z(value, by):
    return lax.ppermute(value, "z", [(z, (z + by) % NZ) for z in range(NZ)])


def shift(value, along, by, cross=False):
    pairs = []
    for x in range(NX):
        for core in range(NC):
            for y in range(NY):
                to = dict(x=x, y=y)
                to[along[core]] = (to[along[core]] + by) % RING
                to_core = 1 - core if cross else core
                pairs.append(((x * NC + core) * NY + y, (to["x"] * NC + to_core) * NY + to["y"]))
    return lax.ppermute(value, ("x", "core", "y"), pairs)


def body(image, variance, patches, offsets, psf_index, coeff_table, basis_taps):
    here = jnp.stack([lax.axis_index(axis) for axis in ("x", "core", "y", "z")]).astype(jnp.int32)
    given = (psf_index, coeff_table.T, basis_taps, patches.transpose(0, 2, 1), offsets.transpose(0, 2, 3, 1),
             image, variance)

    own = [blur_part(part, *given) for part in range(2)]
    left = [shift(a, "yx", 1) for a in own]
    right = [shift(a, "yx", -1) for a in own]
    far = [shift(left[0], "yx", 1), shift(right[1], "yx", -1)]
    held = place(here, own, [(0, 0), (1, 0)])
    held = place(here, (right[0], left[1]), [(0, 1), (1, -1)], held)
    held = place(here, (left[0], right[1]), [(0, -1), (1, 1)], held)
    far, held = lax.optimization_barrier((far, held))
    parts = place(here, far, [(0, 2), (1, 2)], held, last=True)

    stay, stay_cross, far_low, far_high, high, high_cross, low, low_cross, right_low, left_high = parts
    from_left, from_right = shift(far_low, "xy", 1), shift(far_high, "xy", -1)
    high, high_cross = shift(high, "xy", 1), shift(high_cross, "xy", 1, True)
    low, low_cross = shift(low, "xy", -1), shift(low_cross, "xy", -1, True)
    stay_cross = lax.ppermute(stay_cross, "core", [(0, 1), (1, 0)])
    last = add_received(right_low, from_left, left_high, from_right)
    same_low, cross_low = shift(last[0], "xy", 1), shift(last[1], "xy", 1, True)
    same_high, cross_high = shift(last[2], "xy", -1), shift(last[3], "xy", -1, True)
    stay, *sent, four_low, four_high = join(here, stay, stay_cross, low, same_low, high, same_high,
                                            low_cross, cross_low, high_cross, cross_high)

    low, high = shift_z(four_low, 1), shift_z(four_high, -1)
    sent[2], sent[5] = relay(sent[2], sent[5], low, high)
    return finish(here, (stay, *(shift_z(part, steps) for part, steps in zip(sent, STEPS))))[None]


def solution(mesh):
    fine = Mesh(mesh.devices.reshape(NX, NZ, NC, NY), ("x", "z", "core", "y"))
    own = ("x", "z", "core")
    return jax.shard_map(
        body,
        mesh=fine,
        in_specs=(
            P("y", own, None, None),
            P("y", own, None, None),
            P("y", own, None),
            P("y", own, None, None),
            P("y", own),
            P(),
            P(),
        ),
        out_specs=P(own, "y", None),
        check_vma=False,
    )
```

```python
import functools

import jax
import jax.numpy as jnp
from jax import lax
from jax.experimental import pallas as pl
from jax.experimental.pallas import tpu as pltpu
from jax.sharding import Mesh
from jax.sharding import PartitionSpec as P

PIX = 128
PATCH_PIX = 256
TAPS = 21
MARGIN = TAPS // 2
NB = 3
NX, NZ, NC, NY = 4, 8, 2, 4
RING = 4
STRIP = PATCH_PIX // NY
TILES = 24
HALF = 12
UNROLL = 3
META = 8
PATCH, ROW, COL, RANK, WEIGHT = range(5)
ENTRIES = NZ * NC
ENTRY_ROWS = 2 * STRIP
SLOTS = 32
STEPS = (1, 2, 3, -1, -2, -3)
LAST = ((0, 8), (4, 12), (32, 36), (40, 44), (24,), (28,), (48,), (52,), (16, 20), (56, 60))
F32 = jnp.float32
BF16 = jnp.bfloat16
BLUR_LIMIT = 56 * 1024 * 1024
PLACE_LIMIT = 24 * 1024 * 1024
ADD_LIMIT = 12 * 1024 * 1024


def split(value):
    high = value.astype(BF16)
    return high, (value - high.astype(F32)).astype(BF16)


def dot(a, b):
    return jnp.dot(a, b, preferred_element_type=F32)


def blur_kernel(psf_ref, table_ref, taps_ref, patch_ref, offset_ref, img_ref, var_ref, *refs):
    *outs, col_hi, col_lo, rows = refs

    @pl.when(pl.program_id(0) == 0)
    def _():
        major = lax.broadcasted_iota(jnp.int32, (PIX, PIX), 0)
        minor = lax.broadcasted_iota(jnp.int32, (PIX, PIX), 1)
        for b in range(NB):
            lanes = slice(b * PIX, (b + 1) * PIX)
            for axis, diff in ((0, minor - major), (1, major - minor)):
                band = jnp.zeros((PIX, PIX), F32)
                for t in range(TAPS):
                    band = jnp.where(diff == t - MARGIN, taps_ref[b, axis, t], band)
                hi, lo = split(band)
                if axis:
                    col_hi[:PIX, lanes], col_hi[PIX:, lanes], col_lo[:, lanes] = hi, hi, lo
                else:
                    rows[:PIX, lanes], rows[PIX:, lanes] = hi, lo

    def blur(first, out_ref):
        x_hi, x_lo = split(img_ref[0].reshape(HALF * PIX, PIX))
        smooth = dot(jnp.concatenate([x_hi, x_lo], axis=1), col_hi[...]) + dot(x_hi, col_lo[...])
        weights = []
        for n in range(HALF):
            total = jnp.sum(jnp.sum(var_ref[0, n], axis=0, keepdims=True), axis=1, keepdims=True)
            weights.append(1.0 / (total * (1.0 / (PIX * PIX))))
        for pair in range(HALF // 2):
            sides = []
            for n in (2 * pair, 2 * pair + 1):
                row = psf_ref[0, first + n]
                sides.append(jnp.concatenate(
                    [smooth[n * PIX:(n + 1) * PIX, b * PIX:(b + 1) * PIX] * (table_ref[b, row] * weights[n])
                     for b in range(NB)], axis=0))
            q_hi, q_lo = split(jnp.concatenate(sides, axis=1))
            both = dot(rows[...], q_hi)
            done = both[:PIX] + (both[PIX:] + dot(rows[:PIX], q_lo))
            for n in range(2):
                at = META + (2 * pair + n) * PIX
                out_ref[at:at + PIX, :] = done[:, n * PIX:(n + 1) * PIX]

        lane = lax.broadcasted_iota(jnp.int32, (META, PIX), 1)
        kind = lax.broadcasted_iota(jnp.int32, (META, PIX), 0)
        patch, facts = jnp.zeros((META, PIX), jnp.int32), jnp.zeros((META, PIX), jnp.int32)
        for t in range(TILES):
            for k in range(2):
                here = lane == 2 * t + k
                patch = jnp.where(here, patch_ref[0, k, t], patch)
                place = jnp.where(kind == ROW, offset_ref[0, k, 0, t], offset_ref[0, k, 1, t])
                facts = jnp.where(here, place, facts)
        rank = jnp.zeros((META, PIX), jnp.int32)
        for t in range(TILES):
            for k in range(2):
                rank += jnp.where((patch == patch_ref[0, k, t]) & (lane > 2 * t + k), 1, 0)
        facts = jnp.where(kind == PATCH, patch, jnp.where(kind == RANK, rank, facts)).astype(F32)
        for n in range(HALF):
            facts = jnp.where((kind == WEIGHT) & ((lane >> 1) == first + n), weights[n], facts)
        out_ref[0:META, :] = facts

    for part, out in enumerate(outs):
        pl.when(pl.program_id(0) == part)(functools.partial(blur, part * HALF, out))


def blur_tiles(psf_index, table, taps, patches, offsets, image, variance):
    smem = pl.BlockSpec(memory_space=pltpu.SMEM)
    block = pl.BlockSpec((1, HALF, PIX, PIX), lambda i: (0, i, 0, 0))
    rows = META + HALF * PIX
    return pl.pallas_call(
        blur_kernel,
        grid=(TILES // HALF,),
        in_specs=[smem] * 5 + [block, block],
        out_specs=[pl.BlockSpec((rows, PIX), lambda i: (0, 0))] * 2,
        out_shape=[pltpu.VMEM((rows, PIX), F32)] * 2,
        scratch_shapes=[pltpu.VMEM((2 * PIX, NB * PIX), BF16), pltpu.VMEM((PIX, NB * PIX), BF16),
                        pltpu.VMEM((2 * PIX, NB * PIX), BF16)],
        compiler_params=pltpu.CompilerParams(vmem_limit_bytes=BLUR_LIMIT),
        cost_estimate=pl.CostEstimate(flops=TILES * 76 * 10**6, bytes_accessed=TILES * 3 * 65536,
                                      transcendentals=0),
        name="blur_tiles",
    )(psf_index, table, taps, patches, offsets, image, variance)


def place_kernel(runs, held, last, here_ref, *refs):
    count = len(runs)
    tiles, refs = refs[:count], refs[count:]
    if held:
        old_canvas, old_notes, *refs = refs
    *outs, canvas, notes = refs[:-6]
    buf, whole_facts, whole_ref, weight_ref, list_ref, sems = refs[-6:]
    copies, starts, at = [], [], STRIP
    for n, source in enumerate(tiles):
        copies.append(pltpu.make_async_copy(source, buf.at[pl.ds(at, source.shape[0])], sems.at[n]))
        copies[n].start()
        buf[at - STRIP:at] = jnp.zeros((STRIP, PIX), F32)
        starts.append(at + META)
        at += source.shape[0] + STRIP
    buf[at - STRIP:at] = jnp.zeros((STRIP, PIX), F32)
    if held:
        canvas[...] = old_canvas[...]
        notes[...] = old_notes[...]
    else:
        canvas[...] = jnp.zeros(canvas.shape, F32)
        notes[...] = jnp.zeros(notes.shape, F32)
    my_x, core, my_y = here_ref[0], here_ref[1], here_ref[2]
    to_scalars = []
    for n, copy in enumerate(copies):
        copy.wait()
        rows = pl.ds(n * META, META)
        head = pl.ds(starts[n] - META, META)
        whole_facts[n * META:(n + 1) * META] = buf[starts[n] - META:starts[n]].astype(jnp.int32)
        to_scalars.append(pltpu.make_async_copy(whole_facts.at[rows], whole_ref.at[rows], sems.at[count + n]))
        to_scalars.append(pltpu.make_async_copy(buf.at[head], weight_ref.at[rows], sems.at[2 * count + n]))
        for scalars in to_scalars[-2:]:
            scalars.start()
    for scalars in to_scalars:
        scalars.wait()
    row_of = lax.broadcasted_iota(jnp.int32, (8, PIX), 0)
    lane = lax.broadcasted_iota(jnp.int32, (8, PIX), 1)
    lane_one = lax.broadcasted_iota(jnp.int32, (1, PIX), 1)

    def add(items):
        moved = [pltpu.roll(buf[pl.ds(tile_row + skip, STRIP), :], (col + PIX) & (PIX - 1), 1)
                 for _, tile_row, skip, col in items]
        for (at, _, skip, col), strip in zip(items, moved):
            sides = [(lane >= col - n * PIX) & (lane < col - n * PIX + PIX) for n in range(2)]
            for g in range(0, STRIP, 8):
                line = row_of + (skip + g)
                inside = (line >= 0) & (line < PIX)
                for n in range(2):
                    canvas[at, n, g:g + 8] += jnp.where(inside & sides[n], strip[g:g + 8], 0.0)

    def bounded(skip):
        return jnp.clip(skip, -STRIP, PIX)

    def pair_of(index, pair, slot):
        patch, row, col, rank = (whole_ref[index * META + kind, pair] for kind in (PATCH, ROW, COL, RANK))
        weight = weight_ref[index * META + WEIGHT, pair]
        slot = slot + rank
        place = jnp.where(lane_one == slot + SLOTS, row, jnp.where(lane_one == slot + 2 * SLOTS, col, 0))
        return patch, row, col, jnp.where(lane_one == slot, weight, place.astype(F32))

    def entry_of(patch):
        z = (patch >> 1) & (NZ - 1)
        return (z >> 2) * NZ + ((patch & 1) ^ core) * (NZ // 2) + (z & (NZ // 2 - 1))

    def slot_of(reduce_at, source_at):
        return reduce_at * (2 * RING) + (source_at & (RING - 1)) * 2

    def along_y(t, carry, index, pair, base, steps):
        items = []
        for n in range(UNROLL):
            for k in range(2):
                patch, row, col, note = pair_of(index, pair + 2 * (UNROLL * t + n) + k, slot_of(my_x, my_y + steps))
                at = (((patch >> 4) - my_x) & (RING - 1)) * ENTRIES + entry_of(patch)
                notes[pl.ds(at, 1), :] += note
                items.append((at, base + (UNROLL * t + n) * PIX, bounded(my_y * STRIP - row), col))
        add(items)
        return carry

    def list_x(t, number, index, pair, base, steps):
        for n in range(UNROLL):
            for k in range(2):
                lane_of = pair + 2 * (UNROLL * t + n) + k
                list_ref[0, number] = index * PIX + lane_of
                list_ref[1, number] = base + (UNROLL * t + n) * PIX
                list_ref[2, number] = slot_of(my_y, my_x + steps)
                number += jnp.where((whole_ref[index * META + PATCH, lane_of] >> 4) == my_x, 1, 0)
        return number

    def along_x(t, number):
        items = []
        for k in range(2):
            valid = 2 * t + k < number
            at = jnp.minimum(2 * t + k, number - 1)
            code, tile_row, slot = list_ref[0, at], list_ref[1, at], list_ref[2, at]
            patch, row, col, note = pair_of(code >> 7, code & (PIX - 1), jnp.where(valid, slot, PIX))
            for n in range(NY):
                notes[pl.ds(n * ENTRIES + entry_of(patch), 1), :] += note
            for n in range(3):
                strip = (jnp.maximum(row, 0) >> 6) + n
                skip = jnp.where(valid & (strip < NY), bounded(strip * STRIP - row), PIX)
                at = ((strip - my_y) & (RING - 1)) * ENTRIES + entry_of(patch)
                items.append((at, tile_row, skip, col))
        add(items)
        return number

    given = [(HALF // UNROLL, dict(index=n, pair=2 * HALF * part, base=starts[n], steps=steps))
             for n, (part, steps) in enumerate(runs)]

    @pl.when(core == 0)
    def _():
        for groups, run in given:
            lax.fori_loop(0, groups, functools.partial(along_y, **run), 0)

    @pl.when(core == 1)
    def _():
        number = 0
        for groups, run in given:
            number = lax.fori_loop(0, groups, functools.partial(list_x, **run), number)
        lax.fori_loop(0, (number + 1) >> 1, along_x, number)

    if last:
        for out, first in zip(outs, LAST):
            at = 0
            for start in first:
                out[at * ENTRY_ROWS:(at + 4) * ENTRY_ROWS] = canvas[start:start + 4].reshape(4 * ENTRY_ROWS, PIX)
                out[len(first) * 4 * ENTRY_ROWS + at:len(first) * 4 * ENTRY_ROWS + at + 4] = notes[start:start + 4]
                at += 4


def place(here, arrays, runs, old=(), last=False, cost=6):
    smem = pl.BlockSpec(memory_space=pltpu.SMEM)
    hbm = pl.BlockSpec(memory_space=pl.ANY)
    vmem = pl.BlockSpec(memory_space=pltpu.VMEM)
    canvas, notes = (RING * ENTRIES, 2, STRIP, PIX), (RING * ENTRIES, PIX)
    count, rows = len(arrays), sum(a.shape[0] + STRIP for a in arrays) + STRIP
    outs = [canvas, notes]
    if last:
        outs = [(len(first) * 4 * ENTRY_ROWS + 8, PIX) for first in LAST]
    return pl.pallas_call(
        functools.partial(place_kernel, tuple(runs), bool(old), last),
        in_specs=[smem] + [hbm] * count + [vmem] * len(old),
        out_specs=[vmem] * len(outs),
        out_shape=[pltpu.VMEM(shape, F32) for shape in outs],
        scratch_shapes=([pltpu.VMEM(canvas, F32), pltpu.VMEM(notes, F32)] if last else [])
        + [pltpu.VMEM((rows, PIX), F32),
           pltpu.VMEM((count * META, PIX), jnp.int32),
           pltpu.SMEM((count * META, PIX), jnp.int32),
           pltpu.SMEM((count * META, PIX), F32),
           pltpu.SMEM((3, count * 2 * TILES), jnp.int32),
           pltpu.SemaphoreType.DMA((3 * count,))],
        compiler_params=pltpu.CompilerParams(vmem_limit_bytes=PLACE_LIMIT),
        cost_estimate=pl.CostEstimate(flops=10**6, bytes_accessed=cost * 3690000, transcendentals=0),
        name="place",
    )(here, *arrays, *old)


def add_kernel(a, b, c, d, *outs):
    size = 4 * ENTRY_ROWS
    for n, (one, other) in enumerate(((a, b), (c, d))):
        for k in range(2):
            out = outs[2 * n + k]
            out[:size] = one[k * size:(k + 1) * size] + other[k * size:(k + 1) * size]
            rows = slice(2 * size + 4 * k, 2 * size + 4 * k + 4)
            out[size:size + 4] = one[rows] + other[rows]


def add_received(*arrays):
    vmem = pl.BlockSpec(memory_space=pltpu.VMEM)
    return pl.pallas_call(
        add_kernel,
        in_specs=[vmem] * 4,
        out_specs=[vmem] * 4,
        out_shape=[pltpu.VMEM((4 * ENTRY_ROWS + 8, PIX), F32)] * 4,
        compiler_params=pltpu.CompilerParams(vmem_limit_bytes=ADD_LIMIT),
        name="add_received",
    )(*arrays)


def join_kernel(here_ref, stay, stay_cross, *refs):
    arrays, outs, total, note_sums = refs[:8], refs[8:17], refs[17], refs[18]
    core, my_z = here_ref[1], here_ref[3]
    size = 4 * ENTRY_ROWS
    for half in range(2):
        rows = slice(half * size, (half + 1) * size)
        same, cross = arrays[2 * half:2 * half + 2], arrays[4 + 2 * half:6 + 2 * half]
        total[rows] = ((stay[rows] + stay_cross[rows]) + (same[0][:size] + same[1][:size])
                       + (cross[0][:size] + cross[1][:size]))
        head = slice(2 * size + 4 * half, 2 * size + 4 * half + 4)
        for n, (first, rest) in enumerate(((stay, same), (stay_cross, cross))):
            note_sums[8 * n + 4 * half:8 * n + 4 * half + 4] = (
                first[head] + (rest[0][size:size + 4] + rest[1][size:size + 4]))
    kind = lax.broadcasted_iota(jnp.int32, (8, PIX), 0)

    def rows_of(steps, start, count):
        owner = (my_z + steps) & (NZ - 1)
        return total[pl.ds(pl.multiple_of(owner * ENTRY_ROWS + start, 8), count), :]

    def notes_of(steps, row):
        owner = (my_z + steps) & (NZ - 1)
        same, cross = (note_sums[pl.ds(8 * n + owner, 1), :] for n in range(2))
        return jnp.where(kind == row + core, same, jnp.where(kind == row + 1 - core, cross, 0.0))

    for out, steps in zip(outs, (0, *STEPS)):
        out[:ENTRY_ROWS] = rows_of(steps, 0, ENTRY_ROWS)
        out[ENTRY_ROWS:] = notes_of(steps, 0)
    outs[7][...] = rows_of(4, 0, STRIP)
    outs[8][:STRIP] = rows_of(4, STRIP, STRIP)
    outs[8][STRIP:] = notes_of(4, NC)


def join(here, *arrays):
    vmem = pl.BlockSpec(memory_space=pltpu.VMEM)
    rows = [ENTRY_ROWS + 8] * 7 + [STRIP, STRIP + 8]
    return pl.pallas_call(
        join_kernel,
        in_specs=[pl.BlockSpec(memory_space=pltpu.SMEM)] + [vmem] * 10,
        out_specs=[vmem] * 9,
        out_shape=[pltpu.VMEM((n, PIX), F32) for n in rows],
        scratch_shapes=[pltpu.VMEM((NZ * ENTRY_ROWS, PIX), F32), pltpu.VMEM((2 * NZ, PIX), F32)],
        compiler_params=pltpu.CompilerParams(vmem_limit_bytes=ADD_LIMIT),
        name="join",
    )(here, *arrays)


def relay_kernel(ahead, behind, from_left, from_right, ahead_out, behind_out):
    ahead_out[:STRIP] = ahead[:STRIP] + from_left[...]
    ahead_out[STRIP:] = ahead[STRIP:]
    behind_out[:STRIP] = behind[:STRIP]
    behind_out[STRIP:] = behind[STRIP:] + from_right[...]


def relay(*arrays):
    vmem = pl.BlockSpec(memory_space=pltpu.VMEM)
    return pl.pallas_call(
        relay_kernel,
        in_specs=[vmem] * 4,
        out_specs=[vmem] * 2,
        out_shape=[pltpu.VMEM(arrays[0].shape, F32)] * 2,
        compiler_params=pltpu.CompilerParams(vmem_limit_bytes=ADD_LIMIT),
        name="relay",
    )(*arrays)


def finish_kernel(here_ref, *refs):
    *got, out = refs
    my_y = here_ref[2]
    lane = lax.broadcasted_iota(jnp.int32, (1, PIX), 1)
    row_of = lax.broadcasted_iota(jnp.int32, (STRIP, PIX), 0)
    col_of = lax.broadcasted_iota(jnp.int32, (PATCH_PIX, PIX), 0)
    highs, mids, lows, hits = [], [], [], []
    for source in (*got, got[-1]):
        for core in range(NC):
            at = ENTRY_ROWS + core + (NC if len(hits) >= len(got) * NC else 0)
            note = source[at:at + 1, :]
            weight = jnp.where(lane < SLOTS, note, 0.0)
            row = pltpu.roll(note, PIX - SLOTS, 1).astype(jnp.int32) - my_y * STRIP
            col = pltpu.roll(note, PIX - 2 * SLOTS, 1).astype(jnp.int32)
            line, pixel = row_of - row, col_of - col
            hit = (line >= 0) & (line < PIX)
            high, rest = split(weight)
            mid, low = split(weight - high.astype(F32))
            for many, piece in ((highs, high), (mids, mid), (lows, low)):
                many.append(jnp.where(hit, jnp.broadcast_to(piece.astype(F32), hit.shape), 0.0).astype(BF16))
            hits.append(jnp.where((pixel >= 0) & (pixel < PIX), 1.0, 0.0).astype(BF16))
    left = jnp.concatenate([jnp.concatenate(many, axis=1) for many in (highs, mids, lows)], axis=0)
    sums = lax.dot_general(left, jnp.concatenate(hits, axis=1), (((1,), (1,)), ((), ())),
                           preferred_element_type=F32)
    denominator = sums[:STRIP] + (sums[STRIP:2 * STRIP] + sums[2 * STRIP:]) + 1.0
    for side in range(2):
        rows = slice(side * STRIP, (side + 1) * STRIP)
        total = got[0][rows]
        for source in got[1:]:
            total = total + source[rows]
        lanes = slice(side * PIX, (side + 1) * PIX)
        out[:, lanes] = total / denominator[:, lanes]


def finish(here, got):
    vmem = pl.BlockSpec(memory_space=pltpu.VMEM)
    return pl.pallas_call(
        finish_kernel,
        in_specs=[pl.BlockSpec(memory_space=pltpu.SMEM)] + [vmem] * len(got),
        out_specs=vmem,
        out_shape=jax.ShapeDtypeStruct((STRIP, PATCH_PIX), F32),
        compiler_params=pltpu.CompilerParams(vmem_limit_bytes=ADD_LIMIT),
        name="finish",
    )(here, *got)


def shift_z(value, by):
    return lax.ppermute(value, "z", [(z, (z + by) % NZ) for z in range(NZ)])


def shift(value, along, by, cross=False):
    pairs = []
    for x in range(NX):
        for core in range(NC):
            for y in range(NY):
                to = dict(x=x, y=y)
                to[along[core]] = (to[along[core]] + by) % RING
                to_core = 1 - core if cross else core
                pairs.append(((x * NC + core) * NY + y, (to["x"] * NC + to_core) * NY + to["y"]))
    return lax.ppermute(value, ("x", "core", "y"), pairs)


def body(image, variance, patches, offsets, psf_index, coeff_table, basis_taps):
    here = jnp.stack([lax.axis_index(axis) for axis in ("x", "core", "y", "z")]).astype(jnp.int32)
    given = (psf_index, coeff_table.T, basis_taps, patches.transpose(0, 2, 1), offsets.transpose(0, 2, 3, 1),
             image, variance)

    own = blur_tiles(*given)
    left = [shift(a, "yx", 1) for a in own]
    right = [shift(a, "yx", -1) for a in own]
    far = [shift(left[0], "yx", 1), shift(right[1], "yx", -1)]
    held = place(here, own, [(0, 0), (1, 0)])
    held = place(here, (right[0], left[1]), [(0, 1), (1, -1)], held)
    held = place(here, (left[0], right[1]), [(0, -1), (1, 1)], held)
    far, held = lax.optimization_barrier((far, held))
    parts = place(here, far, [(0, 2), (1, 2)], held, last=True)

    stay, stay_cross, far_low, far_high, high, high_cross, low, low_cross, right_low, left_high = parts
    from_left, from_right = shift(far_low, "xy", 1), shift(far_high, "xy", -1)
    high, high_cross = shift(high, "xy", 1), shift(high_cross, "xy", 1, True)
    low, low_cross = shift(low, "xy", -1), shift(low_cross, "xy", -1, True)
    stay_cross = lax.ppermute(stay_cross, "core", [(0, 1), (1, 0)])
    last = add_received(right_low, from_left, left_high, from_right)
    same_low, cross_low = shift(last[0], "xy", 1), shift(last[1], "xy", 1, True)
    same_high, cross_high = shift(last[2], "xy", -1), shift(last[3], "xy", -1, True)
    stay, *sent, four_low, four_high = join(here, stay, stay_cross, low, same_low, high, same_high,
                                            low_cross, cross_low, high_cross, cross_high)

    low, high = shift_z(four_low, 1), shift_z(four_high, -1)
    sent[2], sent[5] = relay(sent[2], sent[5], low, high)
    return finish(here, (stay, *(shift_z(part, steps) for part, steps in zip(sent, STEPS))))[None]


def solution(mesh):
    fine = Mesh(mesh.devices.reshape(NX, NZ, NC, NY), ("x", "z", "core", "y"))
    own = ("x", "z", "core")
    return jax.shard_map(
        body,
        mesh=fine,
        in_specs=(
            P("y", own, None, None),
            P("y", own, None, None),
            P("y", own, None),
            P("y", own, None, None),
            P("y", own),
            P(),
            P(),
        ),
        out_specs=P(own, "y", None),
        check_vma=False,
    )
```

```python
import functools

import jax
import jax.numpy as jnp
from jax import lax
from jax.experimental import pallas as pl
from jax.experimental.pallas import tpu as pltpu
from jax.sharding import Mesh
from jax.sharding import PartitionSpec as P

PIX = 128
PATCH_PIX = 256
TAPS = 21
MARGIN = TAPS // 2
NB = 3
NX, NZ, NC, NY = 4, 8, 2, 4
RING = 4
STRIP = PATCH_PIX // NY
TILES = 24
HALF = 12
UNROLL = 3
META = 8
PATCH, ROW, COL, RANK, WEIGHT = range(5)
ENTRIES = NZ * NC
ENTRY_ROWS = 2 * STRIP
SLOTS = 32
STEPS = (1, 2, 3, -1, -2, -3)
LAST = ((0, 8), (4, 12), (32, 36), (40, 44), (24,), (28,), (48,), (52,), (16, 20), (56, 60))
F32 = jnp.float32
BF16 = jnp.bfloat16
BLUR_LIMIT = 56 * 1024 * 1024
PLACE_LIMIT = 24 * 1024 * 1024
ADD_LIMIT = 12 * 1024 * 1024


def split(value):
    high = value.astype(BF16)
    return high, (value - high.astype(F32)).astype(BF16)


def dot(a, b):
    return jnp.dot(a, b, preferred_element_type=F32)


def blur_kernel(psf_ref, table_ref, taps_ref, patch_ref, offset_ref, img_ref, var_ref, *refs):
    *outs, col_hi, col_lo, rows = refs

    @pl.when(pl.program_id(0) == 0)
    def _():
        major = lax.broadcasted_iota(jnp.int32, (PIX, PIX), 0)
        minor = lax.broadcasted_iota(jnp.int32, (PIX, PIX), 1)
        for b in range(NB):
            lanes = slice(b * PIX, (b + 1) * PIX)
            for axis, diff in ((0, minor - major), (1, major - minor)):
                band = jnp.zeros((PIX, PIX), F32)
                for t in range(TAPS):
                    band = jnp.where(diff == t - MARGIN, taps_ref[b, axis, t], band)
                hi, lo = split(band)
                if axis:
                    col_hi[:PIX, lanes], col_hi[PIX:, lanes], col_lo[:, lanes] = hi, hi, lo
                else:
                    rows[:PIX, lanes], rows[PIX:, lanes] = hi, lo

    def blur(first, out_ref):
        x_hi, x_lo = split(img_ref[0].reshape(HALF * PIX, PIX))
        smooth = dot(jnp.concatenate([x_hi, x_lo], axis=1), col_hi[...]) + dot(x_hi, col_lo[...])
        weights = []
        for n in range(HALF):
            total = jnp.sum(jnp.sum(var_ref[0, n], axis=0, keepdims=True), axis=1, keepdims=True)
            weights.append(1.0 / (total * (1.0 / (PIX * PIX))))
        for pair in range(HALF // 2):
            sides = []
            for n in (2 * pair, 2 * pair + 1):
                row = psf_ref[0, first + n]
                sides.append(jnp.concatenate(
                    [smooth[n * PIX:(n + 1) * PIX, b * PIX:(b + 1) * PIX] * (table_ref[b, row] * weights[n])
                     for b in range(NB)], axis=0))
            q_hi, q_lo = split(jnp.concatenate(sides, axis=1))
            both = dot(rows[...], q_hi)
            done = both[:PIX] + (both[PIX:] + dot(rows[:PIX], q_lo))
            for n in range(2):
                at = META + (2 * pair + n) * PIX
                out_ref[at:at + PIX, :] = done[:, n * PIX:(n + 1) * PIX]

        lane = lax.broadcasted_iota(jnp.int32, (META, PIX), 1)
        kind = lax.broadcasted_iota(jnp.int32, (META, PIX), 0)
        patch, facts = jnp.zeros((META, PIX), jnp.int32), jnp.zeros((META, PIX), jnp.int32)
        for t in range(TILES):
            for k in range(2):
                here = lane == 2 * t + k
                patch = jnp.where(here, patch_ref[0, k, t], patch)
                place = jnp.where(kind == ROW, offset_ref[0, k, 0, t], offset_ref[0, k, 1, t])
                facts = jnp.where(here, place, facts)
        rank = jnp.zeros((META, PIX), jnp.int32)
        for t in range(TILES):
            for k in range(2):
                rank += jnp.where((patch == patch_ref[0, k, t]) & (lane > 2 * t + k), 1, 0)
        facts = jnp.where(kind == PATCH, patch, jnp.where(kind == RANK, rank, facts)).astype(F32)
        for n in range(HALF):
            facts = jnp.where((kind == WEIGHT) & ((lane >> 1) == first + n), weights[n], facts)
        out_ref[0:META, :] = facts

    for part, out in enumerate(outs):
        pl.when(pl.program_id(0) == part)(functools.partial(blur, part * HALF, out))


def blur_tiles(psf_index, table, taps, patches, offsets, image, variance):
    smem = pl.BlockSpec(memory_space=pltpu.SMEM)
    block = pl.BlockSpec((1, HALF, PIX, PIX), lambda i: (0, i, 0, 0))
    rows = META + HALF * PIX
    return pl.pallas_call(
        blur_kernel,
        grid=(TILES // HALF,),
        in_specs=[smem] * 5 + [block, block],
        out_specs=[pl.BlockSpec((rows, PIX), lambda i: (0, 0))] * 2,
        out_shape=[pltpu.VMEM((rows, PIX), F32)] * 2,
        scratch_shapes=[pltpu.VMEM((2 * PIX, NB * PIX), BF16), pltpu.VMEM((PIX, NB * PIX), BF16),
                        pltpu.VMEM((2 * PIX, NB * PIX), BF16)],
        compiler_params=pltpu.CompilerParams(vmem_limit_bytes=BLUR_LIMIT),
        cost_estimate=pl.CostEstimate(flops=TILES * 76 * 10**6, bytes_accessed=TILES * 3 * 65536,
                                      transcendentals=0),
        name="blur_tiles",
    )(psf_index, table, taps, patches, offsets, image, variance)


def place_kernel(runs, held, last, here_ref, *refs):
    count = len(runs)
    tiles, refs = refs[:count], refs[count:]
    if held:
        old_canvas, old_notes, *refs = refs
    *outs, canvas, notes = refs[:-6]
    buf, whole_facts, whole_ref, weight_ref, list_ref, sems = refs[-6:]
    copies, starts, at = [], [], STRIP
    for n, source in enumerate(tiles):
        copies.append(pltpu.make_async_copy(source, buf.at[pl.ds(at, source.shape[0])], sems.at[n]))
        copies[n].start()
        buf[at - STRIP:at] = jnp.zeros((STRIP, PIX), F32)
        starts.append(at + META)
        at += source.shape[0] + STRIP
    buf[at - STRIP:at] = jnp.zeros((STRIP, PIX), F32)
    if held:
        canvas[...] = old_canvas[...]
        notes[...] = old_notes[...]
    else:
        canvas[...] = jnp.zeros(canvas.shape, F32)
        notes[...] = jnp.zeros(notes.shape, F32)
    my_x, core, my_y = here_ref[0], here_ref[1], here_ref[2]
    to_scalars = []
    for n, copy in enumerate(copies):
        copy.wait()
        rows = pl.ds(n * META, META)
        head = pl.ds(starts[n] - META, META)
        whole_facts[n * META:(n + 1) * META] = buf[starts[n] - META:starts[n]].astype(jnp.int32)
        to_scalars.append(pltpu.make_async_copy(whole_facts.at[rows], whole_ref.at[rows], sems.at[count + n]))
        to_scalars.append(pltpu.make_async_copy(buf.at[head], weight_ref.at[rows], sems.at[2 * count + n]))
        for scalars in to_scalars[-2:]:
            scalars.start()
    for scalars in to_scalars:
        scalars.wait()
    row_of = lax.broadcasted_iota(jnp.int32, (8, PIX), 0)
    lane = lax.broadcasted_iota(jnp.int32, (8, PIX), 1)
    lane_one = lax.broadcasted_iota(jnp.int32, (1, PIX), 1)

    def add(items):
        moved = [pltpu.roll(buf[pl.ds(tile_row + skip, STRIP), :], (col + PIX) & (PIX - 1), 1)
                 for _, tile_row, skip, col in items]
        for (at, _, skip, col), strip in zip(items, moved):
            sides = [(lane >= col - n * PIX) & (lane < col - n * PIX + PIX) for n in range(2)]
            for g in range(0, STRIP, 8):
                line = row_of + (skip + g)
                inside = (line >= 0) & (line < PIX)
                for n in range(2):
                    canvas[at, n, g:g + 8] += jnp.where(inside & sides[n], strip[g:g + 8], 0.0)

    def bounded(skip):
        return jnp.clip(skip, -STRIP, PIX)

    def pair_of(index, pair, slot):
        patch, row, col, rank = (whole_ref[index * META + kind, pair] for kind in (PATCH, ROW, COL, RANK))
        weight = weight_ref[index * META + WEIGHT, pair]
        slot = slot + rank
        place = jnp.where(lane_one == slot + SLOTS, row, jnp.where(lane_one == slot + 2 * SLOTS, col, 0))
        return patch, row, col, jnp.where(lane_one == slot, weight, place.astype(F32))

    def entry_of(patch):
        z = (patch >> 1) & (NZ - 1)
        return (z >> 2) * NZ + ((patch & 1) ^ core) * (NZ // 2) + (z & (NZ // 2 - 1))

    def slot_of(reduce_at, source_at):
        return reduce_at * (2 * RING) + (source_at & (RING - 1)) * 2

    def along_y(t, carry, index, pair, base, steps):
        items = []
        for n in range(UNROLL):
            for k in range(2):
                patch, row, col, note = pair_of(index, pair + 2 * (UNROLL * t + n) + k, slot_of(my_x, my_y + steps))
                at = (((patch >> 4) - my_x) & (RING - 1)) * ENTRIES + entry_of(patch)
                notes[pl.ds(at, 1), :] += note
                items.append((at, base + (UNROLL * t + n) * PIX, bounded(my_y * STRIP - row), col))
        add(items)
        return carry

    def list_x(t, number, index, pair, base, steps):
        for n in range(UNROLL):
            for k in range(2):
                lane_of = pair + 2 * (UNROLL * t + n) + k
                list_ref[0, number] = index * PIX + lane_of
                list_ref[1, number] = base + (UNROLL * t + n) * PIX
                list_ref[2, number] = slot_of(my_y, my_x + steps)
                number += jnp.where((whole_ref[index * META + PATCH, lane_of] >> 4) == my_x, 1, 0)
        return number

    def along_x(t, number):
        items = []
        for k in range(2):
            valid = 2 * t + k < number
            at = jnp.minimum(2 * t + k, number - 1)
            code, tile_row, slot = list_ref[0, at], list_ref[1, at], list_ref[2, at]
            patch, row, col, note = pair_of(code >> 7, code & (PIX - 1), jnp.where(valid, slot, PIX))
            for n in range(NY):
                notes[pl.ds(n * ENTRIES + entry_of(patch), 1), :] += note
            for n in range(3):
                strip = (jnp.maximum(row, 0) >> 6) + n
                skip = jnp.where(valid & (strip < NY), bounded(strip * STRIP - row), PIX)
                at = ((strip - my_y) & (RING - 1)) * ENTRIES + entry_of(patch)
                items.append((at, tile_row, skip, col))
        add(items)
        return number

    given = [(HALF // UNROLL, dict(index=n, pair=2 * HALF * part, base=starts[n], steps=steps))
             for n, (part, steps) in enumerate(runs)]

    @pl.when(core == 0)
    def _():
        for groups, run in given:
            lax.fori_loop(0, groups, functools.partial(along_y, **run), 0)

    @pl.when(core == 1)
    def _():
        number = 0
        for groups, run in given:
            number = lax.fori_loop(0, groups, functools.partial(list_x, **run), number)
        lax.fori_loop(0, (number + 1) >> 1, along_x, number)

    if last:
        for out, first in zip(outs, LAST):
            at = 0
            for start in first:
                out[at * ENTRY_ROWS:(at + 4) * ENTRY_ROWS] = canvas[start:start + 4].reshape(4 * ENTRY_ROWS, PIX)
                out[len(first) * 4 * ENTRY_ROWS + at:len(first) * 4 * ENTRY_ROWS + at + 4] = notes[start:start + 4]
                at += 4


def place(here, arrays, runs, old=(), last=False, cost=6):
    smem = pl.BlockSpec(memory_space=pltpu.SMEM)
    hbm = pl.BlockSpec(memory_space=pl.ANY)
    vmem = pl.BlockSpec(memory_space=pltpu.VMEM)
    canvas, notes = (RING * ENTRIES, 2, STRIP, PIX), (RING * ENTRIES, PIX)
    count, rows = len(arrays), sum(a.shape[0] + STRIP for a in arrays) + STRIP
    outs = [canvas, notes]
    if last:
        outs = [(len(first) * 4 * ENTRY_ROWS + 8, PIX) for first in LAST]
    return pl.pallas_call(
        functools.partial(place_kernel, tuple(runs), bool(old), last),
        in_specs=[smem] + [hbm] * count + [vmem] * len(old),
        out_specs=[vmem] * len(outs),
        out_shape=[pltpu.VMEM(shape, F32) for shape in outs],
        scratch_shapes=([pltpu.VMEM(canvas, F32), pltpu.VMEM(notes, F32)] if last else [])
        + [pltpu.VMEM((rows, PIX), F32),
           pltpu.VMEM((count * META, PIX), jnp.int32),
           pltpu.SMEM((count * META, PIX), jnp.int32),
           pltpu.SMEM((count * META, PIX), F32),
           pltpu.SMEM((3, count * 2 * TILES), jnp.int32),
           pltpu.SemaphoreType.DMA((3 * count,))],
        compiler_params=pltpu.CompilerParams(vmem_limit_bytes=PLACE_LIMIT),
        cost_estimate=pl.CostEstimate(flops=10**6, bytes_accessed=cost * 3690000, transcendentals=0),
        name="place",
    )(here, *arrays, *old)


def add_kernel(a, b, c, d, *outs):
    size = 4 * ENTRY_ROWS
    for n, (one, other) in enumerate(((a, b), (c, d))):
        for k in range(2):
            out = outs[2 * n + k]
            out[:size] = one[k * size:(k + 1) * size] + other[k * size:(k + 1) * size]
            rows = slice(2 * size + 4 * k, 2 * size + 4 * k + 4)
            out[size:size + 4] = one[rows] + other[rows]


def add_received(*arrays):
    vmem = pl.BlockSpec(memory_space=pltpu.VMEM)
    return pl.pallas_call(
        add_kernel,
        in_specs=[vmem] * 4,
        out_specs=[vmem] * 4,
        out_shape=[pltpu.VMEM((4 * ENTRY_ROWS + 8, PIX), F32)] * 4,
        compiler_params=pltpu.CompilerParams(vmem_limit_bytes=ADD_LIMIT),
        name="add_received",
    )(*arrays)


def join_kernel(here_ref, stay, stay_cross, *refs):
    arrays, outs, total, note_sums = refs[:8], refs[8:17], refs[17], refs[18]
    core, my_z = here_ref[1], here_ref[3]
    size = 4 * ENTRY_ROWS
    for half in range(2):
        rows = slice(half * size, (half + 1) * size)
        same, cross = arrays[2 * half:2 * half + 2], arrays[4 + 2 * half:6 + 2 * half]
        total[rows] = ((stay[rows] + stay_cross[rows]) + (same[0][:size] + same[1][:size])
                       + (cross[0][:size] + cross[1][:size]))
        head = slice(2 * size + 4 * half, 2 * size + 4 * half + 4)
        for n, (first, rest) in enumerate(((stay, same), (stay_cross, cross))):
            note_sums[8 * n + 4 * half:8 * n + 4 * half + 4] = (
                first[head] + (rest[0][size:size + 4] + rest[1][size:size + 4]))
    kind = lax.broadcasted_iota(jnp.int32, (8, PIX), 0)

    def rows_of(steps, start, count):
        owner = (my_z + steps) & (NZ - 1)
        return total[pl.ds(pl.multiple_of(owner * ENTRY_ROWS + start, 8), count), :]

    def notes_of(steps, row):
        owner = (my_z + steps) & (NZ - 1)
        same, cross = (note_sums[pl.ds(8 * n + owner, 1), :] for n in range(2))
        return jnp.where(kind == row + core, same, jnp.where(kind == row + 1 - core, cross, 0.0))

    for out, steps in zip(outs, (0, *STEPS)):
        out[:ENTRY_ROWS] = rows_of(steps, 0, ENTRY_ROWS)
        out[ENTRY_ROWS:] = notes_of(steps, 0)
    outs[7][...] = rows_of(4, 0, STRIP)
    outs[8][:STRIP] = rows_of(4, STRIP, STRIP)
    outs[8][STRIP:] = notes_of(4, NC)


def join(here, *arrays):
    vmem = pl.BlockSpec(memory_space=pltpu.VMEM)
    rows = [ENTRY_ROWS + 8] * 7 + [STRIP, STRIP + 8]
    return pl.pallas_call(
        join_kernel,
        in_specs=[pl.BlockSpec(memory_space=pltpu.SMEM)] + [vmem] * 10,
        out_specs=[vmem] * 9,
        out_shape=[pltpu.VMEM((n, PIX), F32) for n in rows],
        scratch_shapes=[pltpu.VMEM((NZ * ENTRY_ROWS, PIX), F32), pltpu.VMEM((2 * NZ, PIX), F32)],
        compiler_params=pltpu.CompilerParams(vmem_limit_bytes=ADD_LIMIT),
        name="join",
    )(here, *arrays)


def relay_kernel(ahead, behind, from_left, from_right, ahead_out, behind_out):
    ahead_out[:STRIP] = ahead[:STRIP] + from_left[...]
    ahead_out[STRIP:] = ahead[STRIP:]
    behind_out[:STRIP] = behind[:STRIP]
    behind_out[STRIP:] = behind[STRIP:] + from_right[...]


def relay(*arrays):
    vmem = pl.BlockSpec(memory_space=pltpu.VMEM)
    return pl.pallas_call(
        relay_kernel,
        in_specs=[vmem] * 4,
        out_specs=[vmem] * 2,
        out_shape=[pltpu.VMEM(arrays[0].shape, F32)] * 2,
        compiler_params=pltpu.CompilerParams(vmem_limit_bytes=ADD_LIMIT),
        name="relay",
    )(*arrays)


def sums_of(here_ref, sources):
    my_y = here_ref[2]
    lane = lax.broadcasted_iota(jnp.int32, (1, PIX), 1)
    row_of = lax.broadcasted_iota(jnp.int32, (STRIP, PIX), 0)
    col_of = lax.broadcasted_iota(jnp.int32, (PATCH_PIX, PIX), 0)
    lines = [source[n:n + 1, :] for source, start, stop in sources for n in range(start, stop)]
    pieces, hits = [], []
    for first in range(0, len(lines), PIX // SLOTS):
        weight, row, col = (sum(
            pltpu.roll(jnp.where((lane >= kind * SLOTS) & (lane < (kind + 1) * SLOTS), note, 0.0),
                       (n - kind) * SLOTS % PIX, 1) if n != kind else
            jnp.where((lane >= kind * SLOTS) & (lane < (kind + 1) * SLOTS), note, 0.0)
            for n, note in enumerate(lines[first:first + PIX // SLOTS])) for kind in range(3))
        line = row_of + my_y * STRIP - row.astype(jnp.int32)
        pixel = col_of - col.astype(jnp.int32)
        hit = (line >= 0) & (line < PIX)
        high, rest = split(weight)
        mid, low = split(weight - high.astype(F32))
        pieces.append(jnp.concatenate(
            [jnp.where(hit, jnp.broadcast_to(piece.astype(F32), hit.shape), 0.0).astype(BF16)
             for piece in (high, mid, low)], axis=0))
        hits.append(jnp.where((pixel >= 0) & (pixel < PIX), 1.0, 0.0).astype(BF16))
    sums = lax.dot_general(jnp.concatenate(pieces, axis=1), jnp.concatenate(hits, axis=1),
                           (((1,), (1,)), ((), ())), preferred_element_type=F32)
    total = sources[0][0][:ENTRY_ROWS]
    for source, _, _ in sources[1:]:
        total = total + source[:ENTRY_ROWS]
    return total, sums[:STRIP] + (sums[STRIP:2 * STRIP] + sums[2 * STRIP:])


def begin_kernel(here_ref, *refs):
    *got, numerator, denominator = refs
    numerator[...], denominator[...] = sums_of(here_ref, [(a, ENTRY_ROWS, ENTRY_ROWS + NC) for a in got])


def finish_kernel(here_ref, numerator, denominator, ahead, behind, out):
    total, sums = sums_of(here_ref, ((ahead, ENTRY_ROWS, ENTRY_ROWS + NC), (behind, ENTRY_ROWS, ENTRY_ROWS + 2 * NC)))
    total, sums = total + numerator[...], sums + denominator[...] + 1.0
    for side in range(2):
        lanes = slice(side * PIX, (side + 1) * PIX)
        out[:, lanes] = total[side * STRIP:(side + 1) * STRIP] / sums[:, lanes]


def finish(here, early, late):
    smem = pl.BlockSpec(memory_space=pltpu.SMEM)
    vmem = pl.BlockSpec(memory_space=pltpu.VMEM)
    held = pl.pallas_call(
        begin_kernel,
        in_specs=[smem] + [vmem] * len(early),
        out_specs=[vmem] * 2,
        out_shape=[pltpu.VMEM((ENTRY_ROWS, PIX), F32), pltpu.VMEM((STRIP, PATCH_PIX), F32)],
        compiler_params=pltpu.CompilerParams(vmem_limit_bytes=ADD_LIMIT),
        name="begin",
    )(here, *early)
    return pl.pallas_call(
        finish_kernel,
        in_specs=[smem] + [vmem] * 4,
        out_specs=vmem,
        out_shape=jax.ShapeDtypeStruct((STRIP, PATCH_PIX), F32),
        compiler_params=pltpu.CompilerParams(vmem_limit_bytes=ADD_LIMIT),
        name="finish",
    )(here, *held, *late)


def shift_z(value, by):
    return lax.ppermute(value, "z", [(z, (z + by) % NZ) for z in range(NZ)])


def shift(value, along, by, cross=False):
    pairs = []
    for x in range(NX):
        for core in range(NC):
            for y in range(NY):
                to = dict(x=x, y=y)
                to[along[core]] = (to[along[core]] + by) % RING
                to_core = 1 - core if cross else core
                pairs.append(((x * NC + core) * NY + y, (to["x"] * NC + to_core) * NY + to["y"]))
    return lax.ppermute(value, ("x", "core", "y"), pairs)


def body(image, variance, patches, offsets, psf_index, coeff_table, basis_taps):
    here = jnp.stack([lax.axis_index(axis) for axis in ("x", "core", "y", "z")]).astype(jnp.int32)
    given = (psf_index, coeff_table.T, basis_taps, patches.transpose(0, 2, 1), offsets.transpose(0, 2, 3, 1),
             image, variance)

    own = blur_tiles(*given)
    left = [shift(a, "yx", 1) for a in own]
    right = [shift(a, "yx", -1) for a in own]
    far = [shift(left[0], "yx", 1), shift(right[1], "yx", -1)]
    held = place(here, own, [(0, 0), (1, 0)])
    held = place(here, (right[0], left[1]), [(0, 1), (1, -1)], held)
    held = place(here, (left[0], right[1]), [(0, -1), (1, 1)], held)
    far, held = lax.optimization_barrier((far, held))
    parts = place(here, far, [(0, 2), (1, 2)], held, last=True)

    stay, stay_cross, far_low, far_high, high, high_cross, low, low_cross, right_low, left_high = parts
    from_left, from_right = shift(far_low, "xy", 1), shift(far_high, "xy", -1)
    high, high_cross = shift(high, "xy", 1), shift(high_cross, "xy", 1, True)
    low, low_cross = shift(low, "xy", -1), shift(low_cross, "xy", -1, True)
    stay_cross = lax.ppermute(stay_cross, "core", [(0, 1), (1, 0)])
    last = add_received(right_low, from_left, left_high, from_right)
    same_low, cross_low = shift(last[0], "xy", 1), shift(last[1], "xy", 1, True)
    same_high, cross_high = shift(last[2], "xy", -1), shift(last[3], "xy", -1, True)
    stay, *sent, four_low, four_high = join(here, stay, stay_cross, low, same_low, high, same_high,
                                            low_cross, cross_low, high_cross, cross_high)

    low, high = shift_z(four_low, 1), shift_z(four_high, -1)
    sent[2], sent[5] = relay(sent[2], sent[5], low, high)
    got = [shift_z(part, steps) for part, steps in zip(sent, STEPS)]
    return finish(here, (stay, got[0], got[1], got[3], got[4]), (got[2], got[5]))[None]


def solution(mesh):
    fine = Mesh(mesh.devices.reshape(NX, NZ, NC, NY), ("x", "z", "core", "y"))
    own = ("x", "z", "core")
    return jax.shard_map(
        body,
        mesh=fine,
        in_specs=(
            P("y", own, None, None),
            P("y", own, None, None),
            P("y", own, None),
            P("y", own, None, None),
            P("y", own),
            P(),
            P(),
        ),
        out_specs=P(own, "y", None),
        check_vma=False,
    )
```

```python
import functools

import jax
import jax.numpy as jnp
from jax import lax
from jax.experimental import pallas as pl
from jax.experimental.pallas import tpu as pltpu
from jax.sharding import Mesh
from jax.sharding import PartitionSpec as P

PIX = 128
PATCH_PIX = 256
TAPS = 21
MARGIN = TAPS // 2
NB = 3
NX, NZ, NC, NY = 4, 8, 2, 4
RING = 4
STRIP = PATCH_PIX // NY
TILES = 24
HALF = 12
UNROLL = 6
LISTED = 4
META = 8
PATCH, ROW, COL, RANK, WEIGHT = range(5)
ENTRIES = NZ * NC
ENTRY_ROWS = 2 * STRIP
SLOTS = 32
STEPS = (1, 2, 3, -1, -2, -3)
LAST = ((0, 8), (4, 12), (32, 36), (40, 44), (24,), (28,), (48,), (52,), (16, 20), (56, 60))
F32 = jnp.float32
BF16 = jnp.bfloat16
BLUR_LIMIT = 56 * 1024 * 1024
PLACE_LIMIT = 24 * 1024 * 1024
ADD_LIMIT = 12 * 1024 * 1024


def split(value):
    high = value.astype(BF16)
    return high, (value - high.astype(F32)).astype(BF16)


def dot(a, b):
    return jnp.dot(a, b, preferred_element_type=F32)


def blur_kernel(psf_ref, table_ref, taps_ref, patch_ref, offset_ref, img_ref, var_ref, *refs):
    *outs, col_hi, col_lo, rows = refs

    @pl.when(pl.program_id(0) == 0)
    def _():
        major = lax.broadcasted_iota(jnp.int32, (PIX, PIX), 0)
        minor = lax.broadcasted_iota(jnp.int32, (PIX, PIX), 1)
        for b in range(NB):
            lanes = slice(b * PIX, (b + 1) * PIX)
            for axis, diff in ((0, minor - major), (1, major - minor)):
                band = jnp.zeros((PIX, PIX), F32)
                for t in range(TAPS):
                    band = jnp.where(diff == t - MARGIN, taps_ref[b, axis, t], band)
                hi, lo = split(band)
                if axis:
                    col_hi[:PIX, lanes], col_hi[PIX:, lanes], col_lo[:, lanes] = hi, hi, lo
                else:
                    rows[:PIX, lanes], rows[PIX:, lanes] = hi, lo

    def blur(first, out_ref):
        x_hi, x_lo = split(img_ref[0].reshape(HALF * PIX, PIX))
        smooth = dot(jnp.concatenate([x_hi, x_lo], axis=1), col_hi[...]) + dot(x_hi, col_lo[...])
        weights = []
        for n in range(HALF):
            total = jnp.sum(jnp.sum(var_ref[0, n], axis=0, keepdims=True), axis=1, keepdims=True)
            weights.append(1.0 / (total * (1.0 / (PIX * PIX))))
        for pair in range(HALF // 2):
            sides = []
            for n in (2 * pair, 2 * pair + 1):
                row = psf_ref[0, first + n]
                sides.append(jnp.concatenate(
                    [smooth[n * PIX:(n + 1) * PIX, b * PIX:(b + 1) * PIX] * (table_ref[b, row] * weights[n])
                     for b in range(NB)], axis=0))
            q_hi, q_lo = split(jnp.concatenate(sides, axis=1))
            both = dot(rows[...], q_hi)
            done = both[:PIX] + (both[PIX:] + dot(rows[:PIX], q_lo))
            for n in range(2):
                at = META + (2 * pair + n) * PIX
                out_ref[at:at + PIX, :] = done[:, n * PIX:(n + 1) * PIX]

        lane = lax.broadcasted_iota(jnp.int32, (META, PIX), 1)
        kind = lax.broadcasted_iota(jnp.int32, (META, PIX), 0)
        patch, facts = jnp.zeros((META, PIX), jnp.int32), jnp.zeros((META, PIX), jnp.int32)
        for t in range(TILES):
            for k in range(2):
                here = lane == 2 * t + k
                patch = jnp.where(here, patch_ref[0, k, t], patch)
                place = jnp.where(kind == ROW, offset_ref[0, k, 0, t], offset_ref[0, k, 1, t])
                facts = jnp.where(here, place, facts)
        rank = jnp.zeros((META, PIX), jnp.int32)
        for t in range(TILES):
            for k in range(2):
                rank += jnp.where((patch == patch_ref[0, k, t]) & (lane > 2 * t + k), 1, 0)
        facts = jnp.where(kind == PATCH, patch, jnp.where(kind == RANK, rank, facts)).astype(F32)
        for n in range(HALF):
            facts = jnp.where((kind == WEIGHT) & ((lane >> 1) == first + n), weights[n], facts)
        out_ref[0:META, :] = facts

    for part, out in enumerate(outs):
        pl.when(pl.program_id(0) == part)(functools.partial(blur, part * HALF, out))


def blur_tiles(psf_index, table, taps, patches, offsets, image, variance):
    smem = pl.BlockSpec(memory_space=pltpu.SMEM)
    block = pl.BlockSpec((1, HALF, PIX, PIX), lambda i: (0, i, 0, 0))
    rows = META + HALF * PIX
    return pl.pallas_call(
        blur_kernel,
        grid=(TILES // HALF,),
        in_specs=[smem] * 5 + [block, block],
        out_specs=[pl.BlockSpec((rows, PIX), lambda i: (0, 0))] * 2,
        out_shape=[pltpu.VMEM((rows, PIX), F32)] * 2,
        scratch_shapes=[pltpu.VMEM((2 * PIX, NB * PIX), BF16), pltpu.VMEM((PIX, NB * PIX), BF16),
                        pltpu.VMEM((2 * PIX, NB * PIX), BF16)],
        compiler_params=pltpu.CompilerParams(vmem_limit_bytes=BLUR_LIMIT),
        cost_estimate=pl.CostEstimate(flops=TILES * 76 * 10**6, bytes_accessed=TILES * 3 * 65536,
                                      transcendentals=0),
        name="blur_tiles",
    )(psf_index, table, taps, patches, offsets, image, variance)


def place_kernel(runs, held, last, here_ref, *refs):
    count = len(runs)
    tiles, refs = refs[:count], refs[count:]
    if held:
        old_canvas, old_notes, *refs = refs
    *outs, canvas, notes = refs[:-6]
    buf, whole_facts, whole_ref, weight_ref, list_ref, sems = refs[-6:]
    copies, starts, at = [], [], STRIP
    for n, source in enumerate(tiles):
        copies.append(pltpu.make_async_copy(source, buf.at[pl.ds(at, source.shape[0])], sems.at[n]))
        copies[n].start()
        buf[at - STRIP:at] = jnp.zeros((STRIP, PIX), F32)
        starts.append(at + META)
        at += source.shape[0] + STRIP
    buf[at - STRIP:at] = jnp.zeros((STRIP, PIX), F32)
    if held:
        canvas[...] = old_canvas[...]
        notes[...] = old_notes[...]
    else:
        canvas[...] = jnp.zeros(canvas.shape, F32)
        notes[...] = jnp.zeros(notes.shape, F32)
    my_x, core, my_y = here_ref[0], here_ref[1], here_ref[2]
    to_scalars = []
    for n, copy in enumerate(copies):
        copy.wait()
        rows = pl.ds(n * META, META)
        head = pl.ds(starts[n] - META, META)
        whole_facts[n * META:(n + 1) * META] = buf[starts[n] - META:starts[n]].astype(jnp.int32)
        to_scalars.append(pltpu.make_async_copy(whole_facts.at[rows], whole_ref.at[rows], sems.at[count + n]))
        to_scalars.append(pltpu.make_async_copy(buf.at[head], weight_ref.at[rows], sems.at[2 * count + n]))
        for scalars in to_scalars[-2:]:
            scalars.start()
    for scalars in to_scalars:
        scalars.wait()
    row_of = lax.broadcasted_iota(jnp.int32, (8, PIX), 0)
    lane = lax.broadcasted_iota(jnp.int32, (8, PIX), 1)
    lane_one = lax.broadcasted_iota(jnp.int32, (1, PIX), 1)

    def add(items):
        moved = [pltpu.roll(buf[pl.ds(tile_row + skip, STRIP), :], (col + PIX) & (PIX - 1), 1)
                 for _, tile_row, skip, col in items]
        for (at, _, skip, col), strip in zip(items, moved):
            sides = [(lane >= col - n * PIX) & (lane < col - n * PIX + PIX) for n in range(2)]
            for g in range(0, STRIP, 8):
                line = row_of + (skip + g)
                inside = (line >= 0) & (line < PIX)
                for n in range(2):
                    canvas[at, n, g:g + 8] += jnp.where(inside & sides[n], strip[g:g + 8], 0.0)

    def bounded(skip):
        return jnp.clip(skip, -STRIP, PIX)

    def pair_of(index, pair, slot):
        patch, row, col, rank = (whole_ref[index * META + kind, pair] for kind in (PATCH, ROW, COL, RANK))
        weight = weight_ref[index * META + WEIGHT, pair]
        slot = slot + rank
        place = jnp.where(lane_one == slot + SLOTS, row, jnp.where(lane_one == slot + 2 * SLOTS, col, 0))
        return patch, row, col, jnp.where(lane_one == slot, weight, place.astype(F32))

    def entry_of(patch):
        z = (patch >> 1) & (NZ - 1)
        return (z >> 2) * NZ + ((patch & 1) ^ core) * (NZ // 2) + (z & (NZ // 2 - 1))

    def slot_of(reduce_at, source_at):
        return reduce_at * (2 * RING) + (source_at & (RING - 1)) * 2

    def along_y(t, carry, index, pair, base, steps):
        items = []
        for n in range(UNROLL):
            for k in range(2):
                patch, row, col, note = pair_of(index, pair + 2 * (UNROLL * t + n) + k, slot_of(my_x, my_y + steps))
                at = (((patch >> 4) - my_x) & (RING - 1)) * ENTRIES + entry_of(patch)
                notes[pl.ds(at, 1), :] += note
                items.append((at, base + (UNROLL * t + n) * PIX, bounded(my_y * STRIP - row), col))
        add(items)
        return carry

    def list_x(t, number, index, pair, base, steps):
        for n in range(UNROLL):
            for k in range(2):
                lane_of = pair + 2 * (UNROLL * t + n) + k
                list_ref[0, number] = index * PIX + lane_of
                list_ref[1, number] = base + (UNROLL * t + n) * PIX
                list_ref[2, number] = slot_of(my_y, my_x + steps)
                number += jnp.where((whole_ref[index * META + PATCH, lane_of] >> 4) == my_x, 1, 0)
        return number

    def along_x(t, number):
        items = []
        for k in range(LISTED):
            valid = LISTED * t + k < number
            at = jnp.minimum(LISTED * t + k, number - 1)
            code, tile_row, slot = list_ref[0, at], list_ref[1, at], list_ref[2, at]
            patch, row, col, note = pair_of(code >> 7, code & (PIX - 1), jnp.where(valid, slot, PIX))
            for n in range(NY):
                notes[pl.ds(n * ENTRIES + entry_of(patch), 1), :] += note
            for n in range(3):
                strip = (jnp.maximum(row, 0) >> 6) + n
                skip = jnp.where(valid & (strip < NY), bounded(strip * STRIP - row), PIX)
                at = ((strip - my_y) & (RING - 1)) * ENTRIES + entry_of(patch)
                items.append((at, tile_row, skip, col))
        add(items)
        return number

    given = [(HALF // UNROLL, dict(index=n, pair=2 * HALF * part, base=starts[n], steps=steps))
             for n, (part, steps) in enumerate(runs)]

    @pl.when(core == 0)
    def _():
        for groups, run in given:
            lax.fori_loop(0, groups, functools.partial(along_y, **run), 0)

    @pl.when(core == 1)
    def _():
        number = 0
        for groups, run in given:
            number = lax.fori_loop(0, groups, functools.partial(list_x, **run), number)
        lax.fori_loop(0, (number + LISTED - 1) // LISTED, along_x, number)

    if last:
        for out, first in zip(outs, LAST):
            at = 0
            for start in first:
                out[at * ENTRY_ROWS:(at + 4) * ENTRY_ROWS] = canvas[start:start + 4].reshape(4 * ENTRY_ROWS, PIX)
                out[len(first) * 4 * ENTRY_ROWS + at:len(first) * 4 * ENTRY_ROWS + at + 4] = notes[start:start + 4]
                at += 4


def place(here, arrays, runs, old=(), last=False, cost=6):
    smem = pl.BlockSpec(memory_space=pltpu.SMEM)
    hbm = pl.BlockSpec(memory_space=pl.ANY)
    vmem = pl.BlockSpec(memory_space=pltpu.VMEM)
    canvas, notes = (RING * ENTRIES, 2, STRIP, PIX), (RING * ENTRIES, PIX)
    count, rows = len(arrays), sum(a.shape[0] + STRIP for a in arrays) + STRIP
    outs = [canvas, notes]
    if last:
        outs = [(len(first) * 4 * ENTRY_ROWS + 8, PIX) for first in LAST]
    return pl.pallas_call(
        functools.partial(place_kernel, tuple(runs), bool(old), last),
        in_specs=[smem] + [hbm] * count + [vmem] * len(old),
        out_specs=[vmem] * len(outs),
        out_shape=[pltpu.VMEM(shape, F32) for shape in outs],
        scratch_shapes=([pltpu.VMEM(canvas, F32), pltpu.VMEM(notes, F32)] if last else [])
        + [pltpu.VMEM((rows, PIX), F32),
           pltpu.VMEM((count * META, PIX), jnp.int32),
           pltpu.SMEM((count * META, PIX), jnp.int32),
           pltpu.SMEM((count * META, PIX), F32),
           pltpu.SMEM((3, count * 2 * TILES), jnp.int32),
           pltpu.SemaphoreType.DMA((3 * count,))],
        compiler_params=pltpu.CompilerParams(vmem_limit_bytes=PLACE_LIMIT),
        cost_estimate=pl.CostEstimate(flops=10**6, bytes_accessed=cost * 3690000, transcendentals=0),
        name="place",
    )(here, *arrays, *old)


def add_kernel(a, b, c, d, *outs):
    size = 4 * ENTRY_ROWS
    for n, (one, other) in enumerate(((a, b), (c, d))):
        for k in range(2):
            out = outs[2 * n + k]
            out[:size] = one[k * size:(k + 1) * size] + other[k * size:(k + 1) * size]
            rows = slice(2 * size + 4 * k, 2 * size + 4 * k + 4)
            out[size:size + 4] = one[rows] + other[rows]


def add_received(*arrays):
    vmem = pl.BlockSpec(memory_space=pltpu.VMEM)
    return pl.pallas_call(
        add_kernel,
        in_specs=[vmem] * 4,
        out_specs=[vmem] * 4,
        out_shape=[pltpu.VMEM((4 * ENTRY_ROWS + 8, PIX), F32)] * 4,
        compiler_params=pltpu.CompilerParams(vmem_limit_bytes=ADD_LIMIT),
        name="add_received",
    )(*arrays)


def join_kernel(here_ref, stay, stay_cross, *refs):
    arrays, outs, total, note_sums = refs[:8], refs[8:17], refs[17], refs[18]
    core, my_z = here_ref[1], here_ref[3]
    size = 4 * ENTRY_ROWS
    for half in range(2):
        rows = slice(half * size, (half + 1) * size)
        same, cross = arrays[2 * half:2 * half + 2], arrays[4 + 2 * half:6 + 2 * half]
        total[rows] = ((stay[rows] + stay_cross[rows]) + (same[0][:size] + same[1][:size])
                       + (cross[0][:size] + cross[1][:size]))
        head = slice(2 * size + 4 * half, 2 * size + 4 * half + 4)
        for n, (first, rest) in enumerate(((stay, same), (stay_cross, cross))):
            note_sums[8 * n + 4 * half:8 * n + 4 * half + 4] = (
                first[head] + (rest[0][size:size + 4] + rest[1][size:size + 4]))
    kind = lax.broadcasted_iota(jnp.int32, (8, PIX), 0)

    def rows_of(steps, start, count):
        owner = (my_z + steps) & (NZ - 1)
        return total[pl.ds(pl.multiple_of(owner * ENTRY_ROWS + start, 8), count), :]

    def notes_of(steps, row):
        owner = (my_z + steps) & (NZ - 1)
        same, cross = (note_sums[pl.ds(8 * n + owner, 1), :] for n in range(2))
        return jnp.where(kind == row + core, same, jnp.where(kind == row + 1 - core, cross, 0.0))

    for out, steps in zip(outs, (0, *STEPS)):
        out[:ENTRY_ROWS] = rows_of(steps, 0, ENTRY_ROWS)
        out[ENTRY_ROWS:] = notes_of(steps, 0)
    outs[7][...] = rows_of(4, 0, STRIP)
    outs[8][:STRIP] = rows_of(4, STRIP, STRIP)
    outs[8][STRIP:] = notes_of(4, NC)


def join(here, *arrays):
    vmem = pl.BlockSpec(memory_space=pltpu.VMEM)
    rows = [ENTRY_ROWS + 8] * 7 + [STRIP, STRIP + 8]
    return pl.pallas_call(
        join_kernel,
        in_specs=[pl.BlockSpec(memory_space=pltpu.SMEM)] + [vmem] * 10,
        out_specs=[vmem] * 9,
        out_shape=[pltpu.VMEM((n, PIX), F32) for n in rows],
        scratch_shapes=[pltpu.VMEM((NZ * ENTRY_ROWS, PIX), F32), pltpu.VMEM((2 * NZ, PIX), F32)],
        compiler_params=pltpu.CompilerParams(vmem_limit_bytes=ADD_LIMIT),
        name="join",
    )(here, *arrays)


def relay_kernel(ahead, behind, from_left, from_right, ahead_out, behind_out):
    ahead_out[:STRIP] = ahead[:STRIP] + from_left[...]
    ahead_out[STRIP:] = ahead[STRIP:]
    behind_out[:STRIP] = behind[:STRIP]
    behind_out[STRIP:] = behind[STRIP:] + from_right[...]


def relay(*arrays):
    vmem = pl.BlockSpec(memory_space=pltpu.VMEM)
    return pl.pallas_call(
        relay_kernel,
        in_specs=[vmem] * 4,
        out_specs=[vmem] * 2,
        out_shape=[pltpu.VMEM(arrays[0].shape, F32)] * 2,
        compiler_params=pltpu.CompilerParams(vmem_limit_bytes=ADD_LIMIT),
        name="relay",
    )(*arrays)


def sums_of(here_ref, sources):
    my_y = here_ref[2]
    lane = lax.broadcasted_iota(jnp.int32, (1, PIX), 1)
    row_of = lax.broadcasted_iota(jnp.int32, (STRIP, PIX), 0)
    col_of = lax.broadcasted_iota(jnp.int32, (PATCH_PIX, PIX), 0)
    lines = [source[n:n + 1, :] for source, start, stop in sources for n in range(start, stop)]
    pieces, hits = [], []
    for first in range(0, len(lines), PIX // SLOTS):
        weight, row, col = (sum(
            pltpu.roll(jnp.where((lane >= kind * SLOTS) & (lane < (kind + 1) * SLOTS), note, 0.0),
                       (n - kind) * SLOTS % PIX, 1) if n != kind else
            jnp.where((lane >= kind * SLOTS) & (lane < (kind + 1) * SLOTS), note, 0.0)
            for n, note in enumerate(lines[first:first + PIX // SLOTS])) for kind in range(3))
        line = row_of + my_y * STRIP - row.astype(jnp.int32)
        pixel = col_of - col.astype(jnp.int32)
        hit = (line >= 0) & (line < PIX)
        high, rest = split(weight)
        mid, low = split(weight - high.astype(F32))
        pieces.append(jnp.concatenate(
            [jnp.where(hit, jnp.broadcast_to(piece.astype(F32), hit.shape), 0.0).astype(BF16)
             for piece in (high, mid, low)], axis=0))
        hits.append(jnp.where((pixel >= 0) & (pixel < PIX), 1.0, 0.0).astype(BF16))
    sums = lax.dot_general(jnp.concatenate(pieces, axis=1), jnp.concatenate(hits, axis=1),
                           (((1,), (1,)), ((), ())), preferred_element_type=F32)
    total = sources[0][0][:ENTRY_ROWS]
    for source, _, _ in sources[1:]:
        total = total + source[:ENTRY_ROWS]
    return total, sums[:STRIP] + (sums[STRIP:2 * STRIP] + sums[2 * STRIP:])


def begin_kernel(here_ref, *refs):
    *got, numerator, denominator = refs
    numerator[...], denominator[...] = sums_of(here_ref, [(a, ENTRY_ROWS, ENTRY_ROWS + NC) for a in got])


def finish_kernel(here_ref, numerator, denominator, ahead, behind, out):
    total, sums = sums_of(here_ref, ((ahead, ENTRY_ROWS, ENTRY_ROWS + NC), (behind, ENTRY_ROWS, ENTRY_ROWS + 2 * NC)))
    total, sums = total + numerator[...], sums + denominator[...] + 1.0
    for side in range(2):
        lanes = slice(side * PIX, (side + 1) * PIX)
        out[:, lanes] = total[side * STRIP:(side + 1) * STRIP] / sums[:, lanes]


def finish(here, early, late):
    smem = pl.BlockSpec(memory_space=pltpu.SMEM)
    vmem = pl.BlockSpec(memory_space=pltpu.VMEM)
    held = pl.pallas_call(
        begin_kernel,
        in_specs=[smem] + [vmem] * len(early),
        out_specs=[vmem] * 2,
        out_shape=[pltpu.VMEM((ENTRY_ROWS, PIX), F32), pltpu.VMEM((STRIP, PATCH_PIX), F32)],
        compiler_params=pltpu.CompilerParams(vmem_limit_bytes=ADD_LIMIT),
        name="begin",
    )(here, *early)
    return pl.pallas_call(
        finish_kernel,
        in_specs=[smem] + [vmem] * 4,
        out_specs=vmem,
        out_shape=jax.ShapeDtypeStruct((STRIP, PATCH_PIX), F32),
        compiler_params=pltpu.CompilerParams(vmem_limit_bytes=ADD_LIMIT),
        name="finish",
    )(here, *held, *late)


def shift_z(value, by):
    return lax.ppermute(value, "z", [(z, (z + by) % NZ) for z in range(NZ)])


def shift(value, along, by, cross=False):
    pairs = []
    for x in range(NX):
        for core in range(NC):
            for y in range(NY):
                to = dict(x=x, y=y)
                to[along[core]] = (to[along[core]] + by) % RING
                to_core = 1 - core if cross else core
                pairs.append(((x * NC + core) * NY + y, (to["x"] * NC + to_core) * NY + to["y"]))
    return lax.ppermute(value, ("x", "core", "y"), pairs)


def body(image, variance, patches, offsets, psf_index, coeff_table, basis_taps):
    here = jnp.stack([lax.axis_index(axis) for axis in ("x", "core", "y", "z")]).astype(jnp.int32)
    given = (psf_index, coeff_table.T, basis_taps, patches.transpose(0, 2, 1), offsets.transpose(0, 2, 3, 1),
             image, variance)

    own = blur_tiles(*given)
    left = [shift(a, "yx", 1) for a in own]
    right = [shift(a, "yx", -1) for a in own]
    far = [shift(left[0], "yx", 1), shift(right[1], "yx", -1)]
    held = place(here, own, [(0, 0), (1, 0)])
    held = place(here, (right[0], left[1]), [(0, 1), (1, -1)], held)
    held = place(here, (left[0], right[1]), [(0, -1), (1, 1)], held)
    far, held = lax.optimization_barrier((far, held))
    parts = place(here, far, [(0, 2), (1, 2)], held, last=True)

    stay, stay_cross, far_low, far_high, high, high_cross, low, low_cross, right_low, left_high = parts
    from_left, from_right = shift(far_low, "xy", 1), shift(far_high, "xy", -1)
    high, high_cross = shift(high, "xy", 1), shift(high_cross, "xy", 1, True)
    low, low_cross = shift(low, "xy", -1), shift(low_cross, "xy", -1, True)
    stay_cross = lax.ppermute(stay_cross, "core", [(0, 1), (1, 0)])
    last = add_received(right_low, from_left, left_high, from_right)
    same_low, cross_low = shift(last[0], "xy", 1), shift(last[1], "xy", 1, True)
    same_high, cross_high = shift(last[2], "xy", -1), shift(last[3], "xy", -1, True)
    stay, *sent, four_low, four_high = join(here, stay, stay_cross, low, same_low, high, same_high,
                                            low_cross, cross_low, high_cross, cross_high)

    low, high = shift_z(four_low, 1), shift_z(four_high, -1)
    sent[2], sent[5] = relay(sent[2], sent[5], low, high)
    got = [shift_z(part, steps) for part, steps in zip(sent, STEPS)]
    return finish(here, (stay, got[0], got[1], got[3], got[4]), (got[2], got[5]))[None]


def solution(mesh):
    fine = Mesh(mesh.devices.reshape(NX, NZ, NC, NY), ("x", "z", "core", "y"))
    own = ("x", "z", "core")
    return jax.shard_map(
        body,
        mesh=fine,
        in_specs=(
            P("y", own, None, None),
            P("y", own, None, None),
            P("y", own, None),
            P("y", own, None, None),
            P("y", own),
            P(),
            P(),
        ),
        out_specs=P(own, "y", None),
        check_vma=False,
    )
```
